256 devices in a mesh: ctx: 32 (over z, x_hi, core), head: 8 (over y, x_lo).
Axes of the slice: x: 4 (x_hi: 2, x_lo: 2; x = x_hi * 2 + x_lo), y: 4, z: 8, core: 2. Of those that a mesh axis runs over, the one named last changes fastest.
Arguments:
- q_nope: bfloat16 [8192, 16384], P('ctx', 'head'), may hold values from -6 to 6
- q_rope: bfloat16 [8192, 8192], P('ctx', 'head'), may hold values from -48 to 48
- latent: bfloat16 [8192, 512], P(('ctx', 'head')), may hold values from -8 to 8
- amax_prior: float32 [512], replicated, may hold values from 0.5 to 4
- k_rope: bfloat16 [64, 8192], P(None, 'ctx'), may hold values from -6 to 6
- w_uk: bfloat16 [128, 128, 512], P('head'), may hold values from -0.5 to 0.5
- w_uv: bfloat16 [128, 512, 128], P('head'), may hold values from -0.25 to 0.25
- seg_ids: int32 [8192], P('ctx'), may hold values from 0 to 63, never falling along the last dimension, each value on 1 to 768 neighbouring positions
Outputs:
- attended: bfloat16 [8192, 16384], P('ctx', 'head')
- latent_amax: float32 [512], replicated
The draws below stay inside these ranges and needn't reach their ends.
Inputs may be any that keep to these rules, and one draw needn't show every extreme that they name: seg_ids never falls along the tokens; each document has 1 to 768 tokens and one has exactly 768.
All inputs are finite; a program needn't handle non-finite values.
Results may differ from the reference program's by a relative error of at most 0.012.
Values may be sent and summed in bfloat16 or wider, within the bound.
A program may use at most 64 MiB of HBM per device.

```python
import math
import jax
import jax.numpy as jnp
import numpy as np
from jax import lax

HEADS = 128
HD = 128
LAT = 512
ROPE = 64
TOK_DEV = 256
TOKENS = 8192
SEGS = 64
N_CTX = 32


def draw_k_rope(key, part):
    own_key = jax.random.fold_in(key, 1)
    values = jnp.clip(jax.random.normal(own_key, (ROPE, TOKENS), jnp.float32), -6.0, 6.0)
    return values.astype(jnp.bfloat16)


def draw_q_rope(key, part):
    own_key = jax.random.fold_in(key, 2)
    values = jnp.clip(jax.random.normal(own_key, (TOKENS, HEADS * ROPE), jnp.float32), -6.0, 6.0)
    return values.astype(jnp.bfloat16)


def level_of(key, shape, pieces, low, largest):
    gain = 1.0
    for axis_at, shards_of in pieces:
        steps = jax.random.uniform(jax.random.fold_in(jax.random.fold_in(key, 6), axis_at), (shards_of,), jnp.float32, low / len(pieces), largest / len(pieces))
        gain = gain * jnp.repeat(jnp.exp(steps), shape[axis_at] // shards_of).reshape((-1,) + (1,) * (len(shape) - 1 - axis_at))
    return gain


def split_up(number_of, total, most, lean):
    portions = [(1 << 20) // math.isqrt(rank ** lean) + 1 for rank in range(2, number_of + 1)]
    surplus, holding = total - most - (number_of - 1), [1] * (number_of - 1)
    while surplus > 0:
        movable = [i for i in range(number_of - 1) if holding[i] < most]
        whole, budget = sum([portions[i] for i in movable]), surplus
        for i in movable:
            more = min(most - holding[i], max(1, budget * portions[i] // whole), surplus)
            holding[i] = holding[i] + more
            surplus = surplus - more
    return np.array([most] + holding)


def ragged(key, number_of, total, reach, slope):
    if number_of == 2:
        one = jax.random.randint(key, (), max(1, total - reach), min(reach, total - 1) + 1)
        return jnp.stack([one, total - one])
    tallies = jnp.asarray(split_up(number_of, total, reach, slope), jnp.int32)
    pairs = (number_of - 1) // 2
    source_of, receiver = tallies[1:1 + 2 * pairs:2], tallies[2:2 + 2 * pairs:2]
    slack = jnp.minimum(source_of - 1, reach - receiver)
    passed = jax.random.randint(jax.random.fold_in(key, 1), (pairs,), 0, 1 << 20) % (slack + 1)
    tallies = tallies.at[1:1 + 2 * pairs:2].set(source_of - passed).at[2:2 + 2 * pairs:2].set(receiver + passed)
    return tallies[jax.random.permutation(jax.random.fold_in(key, 2), number_of)]


def normal_values(key, extent, width, bound, shards=(), kind=jnp.bfloat16):
    values = width * jax.random.normal(key, extent, jnp.float32)
    if shards:
        values = values * level_of(key, extent, shards, -0.22, 0.18)
    return jnp.clip(values, -bound, bound).astype(kind)


def setup_inputs(seed: int = 0) -> dict:
    key_of = jax.random.split(jax.random.key(seed), 9)
    return {
        "q_nope": normal_values(key_of[0], (TOKENS, HEADS * HD), 1.0, 6.0, ((0, 32), (1, 8))),
        "q_rope": draw_q_rope(jax.random.fold_in(key_of[8], 71), 0),
        "latent": normal_values(key_of[2], (TOKENS, LAT), 1.0, 8.0, ((0, 256),)),
        "amax_prior": jnp.clip(jnp.exp(jax.random.uniform(key_of[3], (LAT,), jnp.float32, math.log(0.5), math.log(4.0))), 0.5, 4.0),
        "k_rope": draw_k_rope(jax.random.fold_in(key_of[8], 71), 0),
        "w_uk": normal_values(key_of[5], (HEADS, HD, LAT), HD ** -0.5, 0.5, ((0, 8),)),
        "w_uv": normal_values(key_of[6], (HEADS, LAT, HD), LAT ** -0.5, 0.25, ((0, 8),)),
        "seg_ids": jnp.searchsorted(jnp.cumsum(ragged(key_of[7], SEGS, TOKENS, 3 * TOK_DEV, 1)), jnp.arange(TOKENS), side="right").astype(jnp.int32),
    }


def frequencies(rdim):
    return jnp.exp(jnp.arange(rdim // 2, dtype=jnp.float32) * (-2.0 * math.log(10000.0) / rdim))


def turn_rows(values, angle):
    half = values.shape[-1] // 2
    first = values[..., :half]
    second = values[..., half:]
    cosine = jnp.cos(angle)
    sine = jnp.sin(angle)
    return jnp.concatenate([first * cosine - second * sine, second * cosine + first * sine], axis=-1)


def turn_cols(values, angle):
    half = values.shape[0] // 2
    first = values[:half]
    second = values[half:]
    cosine = jnp.cos(angle)
    sine = jnp.sin(angle)
    return jnp.concatenate([first * cosine - second * sine, second * cosine + first * sine], axis=0)


def positions_of(seg_ids, nseg):
    onehot = (seg_ids[:, None] == jnp.arange(nseg, dtype=jnp.int32)[None, :]).astype(jnp.int32)
    counts = jnp.sum(onehot, axis=0)
    starts = jnp.cumsum(counts) - counts
    return jnp.arange(seg_ids.shape[0], dtype=jnp.int32) - jnp.sum(onehot * starts[None, :], axis=1)


def reference(q_nope, q_rope, latent, amax_prior, k_rope, w_uk, w_uv, seg_ids):
    latent_amax = jnp.max(jnp.abs(latent.astype(jnp.float32)), axis=0)
    latent_scaled = jnp.clip(latent.astype(jnp.float32) / amax_prior[None, :], -1.0, 1.0).astype(jnp.bfloat16)
    positions = positions_of(seg_ids, SEGS)
    angle = positions.astype(jnp.float32)[:, None] * frequencies(ROPE)[None, :]
    k_turned = turn_cols(k_rope.astype(jnp.float32), angle.T).astype(jnp.bfloat16)
    margin = 3 * TOK_DEV
    lat_pad = jnp.concatenate([jnp.zeros((margin, LAT), jnp.bfloat16), latent_scaled], axis=0)
    rope_pad = jnp.concatenate([jnp.zeros((ROPE, margin), jnp.bfloat16), k_turned], axis=1)
    scale = (HD + ROPE) ** -0.5
    w_uk32 = w_uk.astype(jnp.float32)
    w_uv32 = w_uv.astype(jnp.float32)

    def one_block(block):
        start = (block * TOK_DEV).astype(jnp.int32)
        q_part = lax.dynamic_slice_in_dim(q_nope, start, TOK_DEV, 0).reshape(TOK_DEV, HEADS, HD)
        r_part = lax.dynamic_slice_in_dim(q_rope, start, TOK_DEV, 0).reshape(TOK_DEV, HEADS, ROPE)
        q_angle = lax.dynamic_slice_in_dim(angle, start, TOK_DEV, 0)
        q_pos = lax.dynamic_slice_in_dim(positions, start, TOK_DEV, 0)
        keys = lax.dynamic_slice_in_dim(lat_pad, start, 4 * TOK_DEV, 0)
        rkeys = lax.dynamic_slice_in_dim(rope_pad, start, 4 * TOK_DEV, 1)
        q_latent = jnp.einsum("thd,hdc->thc", q_part.astype(jnp.float32), w_uk32)
        q_absorbed = (q_latent * amax_prior[None, None, :]).astype(jnp.bfloat16)
        q_turned = turn_rows(r_part.astype(jnp.float32), q_angle[:, None, :]).astype(jnp.bfloat16)
        scores = (jnp.einsum("thc,kc->thk", q_absorbed.astype(jnp.float32), keys.astype(jnp.float32))
                  + jnp.einsum("thr,rk->thk", q_turned.astype(jnp.float32), rkeys.astype(jnp.float32))) * scale
        q_index = start + jnp.arange(TOK_DEV, dtype=jnp.int32)
        k_index = start - margin + jnp.arange(4 * TOK_DEV, dtype=jnp.int32)
        visible = (k_index[None, :] <= q_index[:, None]) & (k_index[None, :] >= (q_index - q_pos)[:, None])
        scores = jnp.where(visible[:, None, :], scores, -1e30)
        top = jnp.max(scores, axis=-1, keepdims=True)
        exps = jnp.exp(scores - top)
        denom = jnp.sum(exps, axis=-1)
        weights = exps.astype(jnp.bfloat16)
        total = jnp.einsum("thk,kc->thc", weights.astype(jnp.float32), keys.astype(jnp.float32))
        latent_out = (total * amax_prior[None, None, :] / denom[:, :, None]).astype(jnp.bfloat16)
        result = jnp.einsum("thc,hcd->thd", latent_out.astype(jnp.float32), w_uv32).astype(jnp.bfloat16)
        return result.reshape(TOK_DEV, HEADS * HD)

    blocks = lax.map(one_block, jnp.arange(N_CTX, dtype=jnp.int32))
    return blocks.reshape(TOKENS, HEADS * HD), latent_amax
```

```python
import functools
import math

import jax
import jax.numpy as jnp
import numpy as np
from jax import lax
from jax.experimental import pallas as pl
from jax.experimental.pallas import tpu as pltpu
from jax.sharding import PartitionSpec as P

MESH = pl.DeviceIdType.MESH
BF16 = jnp.bfloat16
F32 = jnp.float32
BLOCKS = 4
HIDDEN = -1e30


def tables(tokens, rope, gain):
    half = rope // 2
    freq = np.exp(np.arange(half) * (-2.0 * math.log(10000.0) / rope))
    q_angle = np.arange(tokens)[:, None] * freq[None, :]
    q_cos = np.tile(np.cos(q_angle), (1, 4)).astype(np.float32)
    q_sin = np.tile(np.sin(q_angle), (1, 4)).astype(np.float32)
    k_place = np.arange(BLOCKS * tokens) - (BLOCKS - 1) * tokens
    k_angle = freq[:, None] * k_place[None, :]
    k_cos = (np.cos(k_angle) * gain).astype(np.float32)
    k_sin = (np.sin(k_angle) * gain).astype(np.float32)
    return q_cos, q_sin, k_cos, k_sin


def nt(a, b):
    return lax.dot_general(a, b, (((1,), (1,)), ((), ())), preferred_element_type=F32)


def nn(a, b):
    return jnp.dot(a, b, preferred_element_type=F32)


def kernel(
    n_ctx, n_head, gain,
    latent, prior, k_rope, seg, q_nope, q_rope, w_uk, w_uv, q_cos, q_sin, k_cos, k_sin,
    seen, qn, qx, kt, kx, vals, oldest, uk, uv, amax_out,
    lat, keys, tops, z_tops, prior_v, seg_v, qr, qc, qs, kc, ks, clipped,
    lat_recv, lat_send, ahead_send, keys_recv, keys_send, sib_send, sib_recv,
    tops_recv, tops_send, z_recv, z_send, load,
):
    ctx = lax.axis_index("ctx")
    me = lax.axis_index("head")
    core = lax.rem(ctx, 2)
    sibling = ctx + 1 - 2 * core
    n_z = n_ctx // 4
    z = ctx // 4
    heads, hd, width = uk.shape
    tokens = qn.shape[0]
    rope = k_rope.shape[0]
    rows = latent.shape[0]
    mine = pl.ds(pl.multiple_of(me * rows, rows), rows)

    kind = lax.rem(ctx, 4)
    has1 = ctx >= 2
    has2 = (core == 1) | (ctx >= 2)
    has0 = ctx >= 3
    next2 = ctx + 2 < n_ctx
    next3 = (core == 1) & (ctx + 3 < n_ctx)

    beside = me + 1 - 2 * lax.rem(me, 2)

    def along(h, d):
        return lax.rem(h + 2 * d + n_head, n_head)

    def rows_of(h):
        return pl.ds(pl.multiple_of(h * rows, rows), rows)

    def remote(src, dst, send, recv, c, h):
        return pltpu.make_async_remote_copy(
            src_ref=src, dst_ref=dst, send_sem=send, recv_sem=recv, device_id=(c, h), device_id_type=MESH
        )

    loads = [
        (latent, lat.at[3, mine]), (k_rope, keys.at[3, pl.ds(0, rope)]), (seg, seg_v), (prior, prior_v),
        (q_rope, qr), (q_cos, qc), (q_sin, qs), (k_cos, kc), (k_sin, ks), (w_uk, uk), (w_uv, uv), (q_nope, qn),
    ]
    loading = [pltpu.make_async_copy(src, dst, load.at[i]) for i, (src, dst) in enumerate(loads)]
    for copy in loading:
        copy.start()
    qn_load = loading[11]

    barrier = pltpu.get_barrier_semaphore()

    def greet(c, h):
        pl.semaphore_signal(barrier, inc=1, device_id=(c, h), device_id_type=MESH)

    for h in (beside, along(me, 1), along(me, -1)):
        greet(ctx, h)
    greet(sibling, me)
    for d in (1, 2, 3):
        greet(4 * z + lax.rem(kind + d, 4), me)
    for k in range(1, n_z):
        greet(4 * lax.rem(z + k, n_z) + kind, me)

    @pl.when(has1)
    def _():
        greet(ctx - 2, me)

    @pl.when((core == 0) & has0)
    def _():
        greet(ctx - 3, me)

    loading[0].wait()
    loading[1].wait()
    loading[2].wait()
    keys[3, rope:, :] = jnp.broadcast_to(seg_v[...].astype(F32), (keys.shape[1] - rope, tokens)).astype(BF16)
    for copy in loading[4:9]:
        copy.wait()
    lane = lax.broadcasted_iota(jnp.int32, (tokens, 128), 1)
    docs = lax.rem(lax.broadcasted_iota(jnp.int32, (128, tokens), 0), 64)
    own = (docs == jnp.broadcast_to(seg_v[...], (128, tokens))).astype(F32).T
    i = lax.broadcasted_iota(jnp.int32, (128, 128), 0)
    j = lax.broadcasted_iota(jnp.int32, (128, 128), 1)
    swap = jnp.where((j % 64 < 32) & (i == j + 32), -1.0, jnp.where((j % 64 >= 32) & (i == j - 32), 1.0, 0.0)).astype(BF16)
    cosine, sine = qc[...], qs[...]

    def turn(p, carry):
        raw = qr[:, pl.ds(pl.multiple_of(p * 128, 128), 128)]
        turned = raw.astype(F32) * cosine + nn(raw, swap) * sine
        qx[2 * p] = jnp.where(lane < 64, turned, own).astype(BF16)
        qx[2 * p + 1] = jnp.where(lane < 64, own, turned).astype(BF16)
        return carry

    lax.fori_loop(0, heads // 2, turn, 0)

    for slot, there in ((0, has0), (1, has1), (2, has2)):
        @pl.when(jnp.logical_not(there))
        def _(slot=slot):
            lat[slot] = jnp.zeros((tokens, width), BF16)
            keys[slot] = jnp.full(keys.shape[1:], -1.0, BF16)

    listeners = next2.astype(jnp.int32) + next3.astype(jnp.int32)
    pl.semaphore_wait(barrier, 7 + (n_z - 1) + listeners)

    ahead2 = remote(lat.at[3, mine], lat.at[1, mine], ahead_send.at[0], lat_recv.at[1, me], ctx + 2, me)
    ahead3 = remote(lat.at[3], lat.at[0], ahead_send.at[1], sib_recv.at[0], ctx + 3, me)
    keys2 = remote(keys.at[3], keys.at[1], keys_send.at[0], keys_recv.at[1], ctx + 2, me)
    keys3 = remote(keys.at[3], keys.at[0], keys_send.at[1], keys_recv.at[0], ctx + 3, me)
    keys_own = remote(keys.at[3], keys.at[2], keys_send.at[2], keys_recv.at[2], sibling, me)

    def hand(slot, h, to, i):
        return remote(lat.at[slot, rows_of(h)], lat.at[slot, rows_of(h)], lat_send.at[slot, i], lat_recv.at[slot, h], ctx, to)

    routes = [
        (me, beside), (me, along(me, 1)), (me, along(me, -1)),
        (beside, along(me, 1)), (beside, along(me, -1)),
        (along(me, -1), along(me, 1)), (along(beside, 1), along(me, -1)),
    ]

    def relay(slot, i):
        return hand(slot, *routes[i], i)

    def arrived(slot, h):
        hand(slot, h, beside, 0).wait_recv()

    def begin(slot):
        for i in range(3):
            relay(slot, i).start()

    def go_on(slot):
        arrived(slot, beside)
        relay(slot, 3).start()
        relay(slot, 4).start()
        arrived(slot, along(me, -1))
        relay(slot, 5).start()
        arrived(slot, along(beside, 1))
        relay(slot, 6).start()

    def complete(slot):
        for h in (along(me, 1), along(beside, -1), along(me, 2), along(beside, 2)):
            arrived(slot, h)

    @pl.when(next2)
    def _():
        ahead2.start()

    begin(3)

    @pl.when(next2)
    def _():
        keys2.start()

    @pl.when(next3)
    def _():
        keys3.start()

    @pl.when(core == 0)
    def _():
        keys_own.start()


    go_on(3)

    @pl.when(has1)
    def _():
        ahead2.wait_recv()
        begin(1)

    complete(3)
    pass_own = remote(lat.at[3], lat.at[2], sib_send.at[0], sib_recv.at[2], sibling, me)

    @pl.when(core == 0)
    def _():
        pass_own.start()

    @pl.when(next3)
    def _():
        ahead3.start()

    @pl.when(has1)
    def _():
        go_on(1)

    loading[3].wait()
    limit = prior_v[...].astype(BF16)
    for copy in loading[9:11]:
        copy.wait()

    def project(slot):
        at = pl.ds((slot - 1) * tokens, tokens)
        raw = lat[slot]
        clipped[...] = jnp.clip(raw, -limit, limit)
        def some(g, carry):
            c = clipped[...]
            up = nt(uk[pl.ds(4 * g, 4)].reshape(4 * hd, width), c) * gain
            kt[pl.ds(4 * g, 4), :, at] = up.astype(BF16).reshape(4, hd, tokens)
            for p in range(2):
                h = 4 * g + 2 * p
                both = nn(c, jnp.concatenate([uv[h], uv[h + 1]], axis=1)).astype(BF16)
                vals[h, at, :] = both[:, :hd]
                vals[h + 1, at, :] = both[:, hd:]
            return carry

        lax.fori_loop(0, heads // 4, some, 0)

    def turn_keys(slot):
        at = pl.ds(slot * tokens, tokens)
        a = keys[slot, 0:32, :].astype(F32)
        b = keys[slot, 32:64, :].astype(F32)
        cosine, sine = kc[:, at], ks[:, at]
        turned = jnp.concatenate([a * cosine - b * sine, b * cosine + a * sine], axis=0).astype(BF16)
        doc = jnp.broadcast_to(keys[slot, 64:80, :].astype(F32)[0:1, :], (64, tokens))
        number = lax.broadcasted_iota(jnp.int32, (64, tokens), 0).astype(F32)
        other = jnp.where(doc == number, 0.0, HIDDEN).astype(BF16)
        kx[0, 0:64, at] = turned
        kx[0, 64:128, at] = other
        kx[1, 0:64, at] = other
        kx[1, 64:128, at] = turned

    tops[kind] = jnp.max(jnp.abs(lat[3].astype(F32)), axis=0, keepdims=True)

    def spread_top(d):
        to = 4 * z + lax.rem(kind + d, 4)
        return remote(tops.at[kind], tops.at[kind], tops_send.at[d], tops_recv.at[kind], to, me)

    for d in (1, 2, 3):
        spread_top(d).start()
    project(3)
    turn_keys(3)

    to_core1 = remote(lat.at[1], lat.at[0], sib_send.at[1], sib_recv.at[0], sibling, me)
    to_core0 = remote(lat.at[1], lat.at[2], sib_send.at[1], sib_recv.at[2], sibling, me)
    keys_to_core1 = remote(keys.at[1], keys.at[0], keys_send.at[3], keys_recv.at[0], sibling, me)
    keys_to_core0 = remote(keys.at[1], keys.at[2], keys_send.at[3], keys_recv.at[2], sibling, me)

    @pl.when(has1)
    def _():
        complete(1)
        keys2.wait_recv()

        @pl.when(core == 0)
        def _():
            to_core1.start()
            keys_to_core1.start()

        @pl.when(core == 1)
        def _():
            to_core0.start()
            keys_to_core0.start()

    for d in (1, 2, 3):
        src = lax.rem(kind + d, 4)
        remote(tops.at[src], tops.at[src], tops_send.at[d], tops_recv.at[src], ctx, me).wait_recv()
    z_tops[z] = jnp.max(tops[...], axis=0)

    def spread_z(k):
        to = 4 * lax.rem(z + k, n_z) + kind
        return remote(z_tops.at[z], z_tops.at[z], z_send.at[k], z_recv.at[z], to, me)

    for k in range(1, n_z):
        spread_z(k).start()

    project(1)
    turn_keys(1)

    @pl.when(has2)
    def _():
        pass_own.wait_recv()
        keys_own.wait_recv()

    project(2)
    turn_keys(2)

    @pl.when(has0)
    def _():
        ahead3.wait_recv()
        keys3.wait_recv()

    oldest[...] = jnp.clip(lat[0], -limit, limit)
    turn_keys(0)

    doc = keys[3, 64:80, :].astype(F32)[0:1, 0:1]
    count = jnp.zeros((1, 1), F32)
    for slot in range(3):
        count += (keys[slot, 64:80, :].astype(F32)[0:1, tokens - 1:] == doc).astype(F32)
    seen[...] = jnp.broadcast_to(count, seen.shape)

    for k in range(1, n_z):
        src = lax.rem(z + k, n_z)
        remote(z_tops.at[src], z_tops.at[src], z_send.at[k], z_recv.at[src], ctx, me).wait_recv()
    amax_out[...] = jnp.max(z_tops[...], axis=0)
    qn_load.wait()

    for d in (1, 2, 3):
        spread_top(d).wait_send()
    for k in range(1, n_z):
        spread_z(k).wait_send()
    for i in range(7):
        relay(3, i).wait_send()

    @pl.when(next2)
    def _():
        ahead2.wait_send()
        keys2.wait_send()

    @pl.when(next3)
    def _():
        ahead3.wait_send()
        keys3.wait_send()

    @pl.when(has1)
    def _():
        for i in range(7):
            relay(1, i).wait_send()
        to_core1.wait_send()
        keys_to_core1.wait_send()

    @pl.when(core == 0)
    def _():
        keys_own.wait_send()
        pass_own.wait_send()


def attend(
    gain, seen, qn, qx, kt, kx, vals, oldest, uk, uv, amax, out, amax_out, kt0, vals0, outs, store, amax_store
):
    heads, hd, width = uk.shape
    tokens = qn.shape[0]
    write_amax = pltpu.make_async_copy(amax, amax_out, amax_store)
    write_amax.start()
    count = jnp.max(seen[...]).astype(jnp.int32)
    together = 4
    q_at = lax.broadcasted_iota(jnp.int32, (tokens, tokens), 0)
    k_at = lax.broadcasted_iota(jnp.int32, (tokens, tokens), 1)

    def write(p):
        some = pl.ds(pl.multiple_of(p * together * hd, together * hd), together * hd)
        return pltpu.make_async_copy(outs.at[:, some], out.at[:, some], store.at[p])

    @pl.when(count == 3)
    def _():
        def some(g, carry):
            c = oldest[...]
            up = nt(uk[pl.ds(4 * g, 4)].reshape(4 * hd, width), c) * gain
            kt0[pl.ds(4 * g, 4)] = up.astype(BF16).reshape(4, hd, tokens)
            for p in range(2):
                h = 4 * g + 2 * p
                both = nn(c, jnp.concatenate([uv[h], uv[h + 1]], axis=1)).astype(BF16)
                vals0[h] = both[:, :hd]
                vals0[h + 1] = both[:, hd:]
            return carry

        lax.fori_loop(0, heads // 4, some, 0)

    def with_blocks(blocks):
        past = blocks * tokens

        def group(g, carry):
            for i in range(together):
                h = together * g + i
                e = i % 2
                cols = pl.ds(pl.multiple_of(h * hd, hd), hd)
                q = jnp.concatenate([qn[:, cols], qx[h]], axis=1)
                if blocks == 3:
                    k = jnp.concatenate([kt0[h], kt[h]], axis=1)
                    v = jnp.concatenate([vals0[h], vals[h]], axis=0)
                else:
                    k = kt[h, :, (2 - blocks) * tokens:]
                    v = vals[h, (2 - blocks) * tokens:, :]
                k = jnp.concatenate([k, kx[e, :, (3 - blocks) * tokens:]], axis=0)
                s = nn(q, k)
                own = jnp.where(k_at <= q_at, s[:, past:], HIDDEN)
                s = jnp.concatenate([s[:, :past], own], axis=1) if blocks else own
                w = jnp.exp2(s - jnp.max(s, axis=1, keepdims=True)).astype(BF16)
                o = nn(w, jnp.concatenate([v, jnp.ones((past + tokens, hd), BF16)], axis=1))
                outs[:, cols] = (o[:, :hd] / o[:, hd:]).astype(BF16)
            write(g).start()
            return carry

        lax.fori_loop(0, heads // together, group, 0)

    for blocks in range(4):
        pl.when(count == blocks)(functools.partial(with_blocks, blocks))

    def written(p, carry):
        write(p).wait()
        return carry

    lax.fori_loop(0, heads // together, written, 0)
    write_amax.wait()


def shards(n_ctx, n_head, q_nope, q_rope, latent, amax_prior, k_rope, w_uk, w_uv, seg_ids):
    tokens, columns = q_nope.shape
    heads, hd, width = w_uk.shape
    rope = k_rope.shape[0]
    rows = latent.shape[0]
    gain = math.log2(math.e) * (hd + rope) ** -0.5
    q_cos, q_sin, k_cos, k_sin = tables(tokens, rope, gain)
    n_z = n_ctx // 4
    keys = BLOCKS * tokens
    dma = pltpu.SemaphoreType.DMA
    anywhere = pl.BlockSpec(memory_space=pl.ANY)
    in_vmem = pl.BlockSpec(memory_space=pltpu.VMEM)
    mib = 1024 * 1024
    operands = (
        latent, amax_prior.reshape(1, width), k_rope, seg_ids.reshape(1, tokens), q_nope, q_rope, w_uk, w_uv,
        jnp.asarray(q_cos), jnp.asarray(q_sin), jnp.asarray(k_cos), jnp.asarray(k_sin),
    )
    results = pl.pallas_call(
        functools.partial(kernel, n_ctx, n_head, gain),
        out_shape=(
            pltpu.VMEM((8, 128), F32),
            pltpu.VMEM((tokens, columns), BF16),
            pltpu.VMEM((heads, tokens, 128), BF16),
            pltpu.VMEM((heads, hd, keys - tokens), BF16),
            pltpu.VMEM((2, 128, keys), BF16),
            pltpu.VMEM((heads, keys - tokens, hd), BF16),
            pltpu.VMEM((tokens, width), BF16),
            pltpu.VMEM((heads, hd, width), BF16),
            pltpu.VMEM((heads, width, hd), BF16),
            pltpu.VMEM((1, width), F32),
        ),
        in_specs=[pl.BlockSpec(memory_space=pltpu.HBM)] * 12,
        out_specs=(in_vmem,) * 10,
        scratch_shapes=[
            pltpu.VMEM((BLOCKS, tokens, width), BF16),
            pltpu.VMEM((BLOCKS, rope + 16, tokens), BF16),
            pltpu.VMEM((4, 1, width), F32),
            pltpu.VMEM((n_z, 1, width), F32),
            pltpu.VMEM((1, width), F32),
            pltpu.VMEM((1, tokens), jnp.int32),
            pltpu.VMEM((tokens, heads * rope), BF16),
            pltpu.VMEM(q_cos.shape, F32),
            pltpu.VMEM(q_sin.shape, F32),
            pltpu.VMEM(k_cos.shape, F32),
            pltpu.VMEM(k_sin.shape, F32),
            pltpu.VMEM((tokens, width), BF16),
            dma((BLOCKS, n_head)),
            dma((BLOCKS, 7)),
            dma((2,)),
            dma((BLOCKS,)),
            dma((BLOCKS,)),
            dma((2,)),
            dma((BLOCKS,)),
            dma((4,)),
            dma((4,)),
            dma((n_z,)),
            dma((n_z,)),
            dma((12,)),
        ],
        compiler_params=pltpu.CompilerParams(collective_id=0, has_side_effects=True, vmem_limit_bytes=16 * mib),
        cost_estimate=pl.CostEstimate(flops=4_000_000_000, bytes_accessed=8_000_000, transcendentals=0),
    )(*(pltpu.with_memory_space_constraint(x, pltpu.HBM) for x in operands))
    attended, latent_amax = pl.pallas_call(
        functools.partial(attend, gain),
        out_shape=(jax.ShapeDtypeStruct((tokens, columns), BF16), jax.ShapeDtypeStruct((1, width), F32)),
        in_specs=[in_vmem] * 10,
        out_specs=(anywhere, anywhere),
        scratch_shapes=[
            pltpu.VMEM((heads, hd, tokens), BF16),
            pltpu.VMEM((heads, tokens, hd), BF16),
            pltpu.VMEM((tokens, columns), BF16),
            dma((heads // 2,)),
            dma,
        ],
        compiler_params=pltpu.CompilerParams(vmem_limit_bytes=24 * mib),
        cost_estimate=pl.CostEstimate(flops=10_000_000_000, bytes_accessed=8_000_000, transcendentals=4_194_304),
    )(*(pltpu.with_memory_space_constraint(x, pltpu.VMEM) for x in results))
    return attended, latent_amax.reshape(width)


def solution(mesh):
    placed = (
        P("ctx", "head"),
        P("ctx", "head"),
        P(("ctx", "head"), None),
        P(),
        P(None, "ctx"),
        P("head", None, None),
        P("head", None, None),
        P("ctx"),
    )
    return jax.shard_map(
        functools.partial(shards, mesh.shape["ctx"], mesh.shape["head"]),
        mesh=mesh, in_specs=placed, out_specs=(P("ctx", "head"), P()), check_vma=False,
    )
```

```python
import functools
import math

import jax
import jax.numpy as jnp
import numpy as np
from jax import lax
from jax.experimental import pallas as pl
from jax.experimental.pallas import tpu as pltpu
from jax.sharding import PartitionSpec as P

MESH = pl.DeviceIdType.MESH
BF16 = jnp.bfloat16
F32 = jnp.float32
BLOCKS = 4
HIDDEN = -1e30


def tables(tokens, rope, gain):
    half = rope // 2
    freq = np.exp(np.arange(half) * (-2.0 * math.log(10000.0) / rope))
    q_angle = np.arange(tokens)[:, None] * freq[None, :]
    q_cos = np.tile(np.cos(q_angle), (1, 4)).astype(np.float32)
    q_sin = np.tile(np.sin(q_angle), (1, 4)).astype(np.float32)
    k_place = np.arange(BLOCKS * tokens) - (BLOCKS - 1) * tokens
    k_angle = freq[:, None] * k_place[None, :]
    k_cos = (np.cos(k_angle) * gain).astype(np.float32)
    k_sin = (np.sin(k_angle) * gain).astype(np.float32)
    return q_cos, q_sin, k_cos, k_sin


def nt(a, b):
    return lax.dot_general(a, b, (((1,), (1,)), ((), ())), preferred_element_type=F32)


def nn(a, b):
    return jnp.dot(a, b, preferred_element_type=F32)


def kernel(
    n_ctx, n_head, gain,
    latent, prior, k_rope, seg, q_nope, q_rope, w_uk, w_uv, q_cos, q_sin, k_cos, k_sin,
    seen, qn, qx, kt, kx, vals, oldest, uk, uv, amax_out,
    lat, keys, tops, z_tops, chain, prior_v, seg_v, qr, qc, qs, kc, ks, clipped,
    pair_recv, pair_send, side_recv, side_send, far_recv, far_send, keys_recv, keys_send, sib_send, sib_recv,
    tops_recv, tops_send, z_recv, z_send, chain_recv, chain_send, load,
):
    ctx = lax.axis_index("ctx")
    me = lax.axis_index("head")
    core = lax.rem(ctx, 2)
    sibling = ctx + 1 - 2 * core
    n_z = n_ctx // 4
    z = ctx // 4
    heads, hd, width = uk.shape
    tokens = qn.shape[0]
    rope = k_rope.shape[0]
    rows = latent.shape[0]
    mine = pl.ds(pl.multiple_of(me * rows, rows), rows)

    kind = lax.rem(ctx, 4)
    has1 = ctx >= 2
    has2 = (core == 1) | (ctx >= 2)
    has0 = ctx >= 3
    next2 = ctx + 2 < n_ctx
    next3 = (core == 1) & (ctx + 3 < n_ctx)

    beside = me + 1 - 2 * lax.rem(me, 2)

    def along(h, d):
        return lax.rem(h + 2 * d + n_head, n_head)

    def remote(src, dst, send, recv, c, h):
        return pltpu.make_async_remote_copy(
            src_ref=src, dst_ref=dst, send_sem=send, recv_sem=recv, device_id=(c, h), device_id_type=MESH
        )

    loads = [
        (latent, lat.at[3, mine]), (k_rope, keys.at[3, pl.ds(0, rope)]), (seg, seg_v), (prior, prior_v),
        (q_rope, qr), (q_cos, qc), (q_sin, qs), (k_cos, kc), (k_sin, ks), (w_uk, uk), (w_uv, uv), (q_nope, qn),
    ]
    loading = [pltpu.make_async_copy(src, dst, load.at[i]) for i, (src, dst) in enumerate(loads)]
    for copy in loading[:9]:
        copy.start()
    qn_load = loading[11]

    z_tops[...] = jnp.zeros_like(z_tops)
    barrier = pltpu.get_barrier_semaphore()

    def greet(c, h):
        pl.semaphore_signal(barrier, inc=1, device_id=(c, h), device_id_type=MESH)

    up, down = along(me, 1), along(me, -1)
    for h in (beside, up, down):
        greet(ctx, h)
    for d in (1, 2, 3):
        greet(4 * z + lax.rem(kind + d, 4), me)
    for k in range(1, n_z):
        pl.when(z + k < n_z)(functools.partial(greet, ctx + 4 * k, me))
    pl.when(z > 0)(functools.partial(greet, ctx - 4, me))

    @pl.when(has1)
    def _():
        greet(ctx - 2, me)
        greet(ctx - 2, beside)

    @pl.when((core == 0) & has0)
    def _():
        greet(ctx - 3, me)
        greet(ctx - 3, beside)

    for slot, there in ((0, has0), (1, has1), (2, has2)):
        @pl.when(jnp.logical_not(there))
        def _(slot=slot):
            lat[slot] = jnp.zeros((tokens, width), BF16)
            keys[slot] = jnp.full(keys.shape[1:], -1.0, BF16)

    listeners = 2 * (next2.astype(jnp.int32) + next3.astype(jnp.int32))
    pl.semaphore_wait(barrier, 6 + listeners + z + (z < n_z - 1).astype(jnp.int32))

    def chunk(slot, i, c, h):
        return remote(latent, lat.at[slot, mine], pair_send.at[slot, i], pair_recv.at[slot, i], c, h)

    chunk3 = chunk(3, 1, ctx, beside)
    chunk1 = [chunk(1, 0, ctx + 2, me), chunk(1, 1, ctx + 2, beside)]
    chunk0 = [chunk(0, 0, ctx + 3, me), chunk(0, 1, ctx + 3, beside)]
    keys2 = remote(keys.at[3], keys.at[1], keys_send.at[0], keys_recv.at[1], ctx + 2, me)
    keys3 = remote(keys.at[3], keys.at[0], keys_send.at[1], keys_recv.at[0], ctx + 3, me)
    keys_own = remote(keys.at[3], keys.at[2], keys_send.at[2], keys_recv.at[2], sibling, me)
    chunk3.start()

    @pl.when(next2)
    def _():
        for copy in chunk1:
            copy.start()

    @pl.when(next3)
    def _():
        for copy in chunk0:
            copy.start()

    for copy in loading[9:]:
        copy.start()

    for copy in loading[:9]:
        copy.wait()
    lane = lax.broadcasted_iota(jnp.int32, (tokens, 128), 1)
    docs = lax.rem(lax.broadcasted_iota(jnp.int32, (128, tokens), 0), 64)
    own = (docs == jnp.broadcast_to(seg_v[...], (128, tokens))).astype(F32).T
    i = lax.broadcasted_iota(jnp.int32, (128, 128), 0)
    j = lax.broadcasted_iota(jnp.int32, (128, 128), 1)
    swap = jnp.where((j % 64 < 32) & (i == j + 32), -1.0, jnp.where((j % 64 >= 32) & (i == j - 32), 1.0, 0.0)).astype(BF16)
    cosine, sine = qc[...], qs[...]
    keys[3, rope:, :] = jnp.broadcast_to(seg_v[...].astype(F32), (keys.shape[1] - rope, tokens)).astype(BF16)

    def turn(p, carry):
        raw = qr[:, pl.ds(pl.multiple_of(p * 128, 128), 128)]
        turned = raw.astype(F32) * cosine + nn(raw, swap) * sine
        qx[2 * p] = jnp.where(lane < 64, turned, own).astype(BF16)
        qx[2 * p + 1] = jnp.where(lane < 64, own, turned).astype(BF16)
        return carry

    lax.fori_loop(0, heads // 2, turn, 0)

    def pair_at(h):
        return pl.ds(pl.multiple_of(h // 2 * 2 * rows, 2 * rows), 2 * rows)

    def one_at(h, x):
        return pl.ds(pl.multiple_of((h // 2 * 2 + x) * rows, rows), rows)

    def side(slots, i, to):
        at = lat.at[slots, pair_at(me)]
        return remote(at, at, side_send.at[slots.start, i], side_recv.at[slots.start, i], ctx, to)

    def far(slots, i, h, to):
        at = lat.at[slots, one_at(h, i)]
        return remote(at, at, far_send.at[slots.start, i], far_recv.at[slots.start, i], ctx, to)

    def sides(slots):
        side(slots, 0, up).start()
        side(slots, 1, down).start()

    def passing(slots, piece):
        if slots.start == 3:
            routes = [(core == 0, 3, 2)]
        else:
            routes = [((core == 0) & has1, 1, 0), ((core == 1) & has1, 1, 2)]
        at = [pair_at(me), pair_at(down), pair_at(up), one_at(along(me, 2), 0), one_at(along(me, 2), 1)][piece]
        sems = sib_send.at[slots.start // 3, piece]
        return [
            (there, remote(lat.at[src, at], lat.at[dst, at], sems, sib_recv.at[dst, piece], sibling, me))
            for there, src, dst in routes
        ]

    def pass_on(slots, piece):
        for there, copy in passing(slots, piece):
            pl.when(there)(copy.start)

    def passed(slots):
        for piece in range(5):
            for there, copy in passing(slots, piece):
                pl.when(there)(copy.wait_send)

    def taken(dst):
        for piece in range(5):
            at = [pair_at(me), pair_at(down), pair_at(up), one_at(along(me, 2), 0), one_at(along(me, 2), 1)][piece]
            remote(lat.at[dst, at], lat.at[dst, at], sib_send.at[0, piece], sib_recv.at[dst, piece], sibling, me).wait_recv()

    def fars(slots):
        side(slots, 0, up).wait_recv()
        far(slots, 0, down, up).start()
        side(slots, 1, down).wait_recv()
        far(slots, 1, up, down).start()

    def complete(slots):
        far(slots, 0, down, up).wait_recv()
        far(slots, 1, up, down).wait_recv()

    def sent(slots):
        for i in range(2):
            side(slots, i, up).wait_send()
            far(slots, i, up, up).wait_send()

    own, late = pl.ds(3, 1), pl.ds(1, 1)
    both = pl.ds(0, 2)
    with_oldest = (core == 0) & has0
    without_oldest = has1 & jnp.logical_not(with_oldest)

    def earlier(act):
        @pl.when(with_oldest)
        def _():
            act(both)

        @pl.when(without_oldest)
        def _():
            act(late)

    chunk3.wait_recv()
    sides(own)
    pass_on(own, 0)

    @pl.when(has1)
    def _():
        for copy in chunk1:
            copy.wait_recv()

    @pl.when(with_oldest)
    def _():
        for copy in chunk0:
            copy.wait_recv()

    earlier(sides)
    pass_on(late, 0)

    @pl.when(next2)
    def _():
        keys2.start()

    @pl.when(next3)
    def _():
        keys3.start()

    @pl.when(core == 0)
    def _():
        keys_own.start()

    fars(own)
    pass_on(own, 1)
    pass_on(own, 2)
    earlier(fars)
    pass_on(late, 1)
    pass_on(late, 2)
    complete(own)
    pass_on(own, 3)
    pass_on(own, 4)

    limit = prior_v[...].astype(BF16)
    for copy in loading[9:11]:
        copy.wait()

    def project(slot):
        at = pl.ds((slot - 1) * tokens, tokens)
        raw = lat[slot]
        clipped[...] = jnp.clip(raw, -limit, limit)
        def some(g, carry):
            c = clipped[...]
            up = nt(uk[pl.ds(4 * g, 4)].reshape(4 * hd, width), c) * gain
            kt[pl.ds(4 * g, 4), :, at] = up.astype(BF16).reshape(4, hd, tokens)
            for p in range(2):
                h = 4 * g + 2 * p
                both = nn(c, jnp.concatenate([uv[h], uv[h + 1]], axis=1)).astype(BF16)
                vals[h, at, :] = both[:, :hd]
                vals[h + 1, at, :] = both[:, hd:]
            return carry

        lax.fori_loop(0, heads // 4, some, 0)

    def turn_keys(slot):
        at = pl.ds(slot * tokens, tokens)
        a = keys[slot, 0:32, :].astype(F32)
        b = keys[slot, 32:64, :].astype(F32)
        cosine, sine = kc[:, at], ks[:, at]
        turned = jnp.concatenate([a * cosine - b * sine, b * cosine + a * sine], axis=0).astype(BF16)
        doc = jnp.broadcast_to(keys[slot, 64:80, :].astype(F32)[0:1, :], (64, tokens))
        number = lax.broadcasted_iota(jnp.int32, (64, tokens), 0).astype(F32)
        other = jnp.where(doc == number, 0.0, HIDDEN).astype(BF16)
        kx[0, 0:64, at] = turned
        kx[0, 64:128, at] = other
        kx[1, 0:64, at] = other
        kx[1, 64:128, at] = turned

    tops[kind] = jnp.max(jnp.abs(lat[3].astype(F32)), axis=0, keepdims=True)

    def spread_top(d):
        to = 4 * z + lax.rem(kind + d, 4)
        return remote(tops.at[kind], tops.at[kind], tops_send.at[d], tops_recv.at[kind], to, me)

    for d in (1, 2, 3):
        spread_top(d).start()
    project(3)
    turn_keys(3)

    for d in (1, 2, 3):
        src = lax.rem(kind + d, 4)
        remote(tops.at[src], tops.at[src], tops_send.at[d], tops_recv.at[src], ctx, me).wait_recv()
    z_tops[z] = jnp.max(tops[...], axis=0)

    def spread_z(k):
        return remote(z_tops.at[z], z_tops.at[z], z_send.at[k], z_recv.at[z], ctx - 4 * k, me)

    for k in range(1, n_z):
        pl.when(z - k >= 0)(spread_z(k).start)

    def step():
        return remote(chain.at[1], chain.at[0], chain_send, chain_recv, ctx + 4, me)

    def climb(point):
        @pl.when(jnp.clip(z - n_z // 2, 0, 2) == point)
        def _():
            @pl.when(z == 0)
            def _():
                chain[1] = z_tops[z]

            @pl.when(z > 0)
            def _():
                step().wait_recv()
                chain[1] = jnp.maximum(chain[0], z_tops[z])

            @pl.when(z < n_z - 1)
            def _():
                step().start()

    climb(0)

    keys_on = [
        ((core == 0) & has1, remote(keys.at[1], keys.at[0], keys_send.at[3], keys_recv.at[0], sibling, me)),
        ((core == 1) & has1, remote(keys.at[1], keys.at[2], keys_send.at[3], keys_recv.at[2], sibling, me)),
    ]
    earlier(complete)
    pass_on(late, 3)
    pass_on(late, 4)
    pl.when(has1)(keys2.wait_recv)
    for there, copy in keys_on:
        pl.when(there)(copy.start)
    project(1)
    turn_keys(1)
    climb(1)

    @pl.when(has2)
    def _():
        taken(2)
        keys_own.wait_recv()

    project(2)
    turn_keys(2)
    climb(2)

    @pl.when((core == 1) & has0)
    def _():
        taken(0)

    @pl.when(has0)
    def _():
        keys3.wait_recv()

    oldest[...] = jnp.clip(lat[0], -limit, limit)
    turn_keys(0)

    doc = keys[3, 64:80, :].astype(F32)[0:1, 0:1]
    count = jnp.zeros((1, 1), F32)
    for slot in range(3):
        count += (keys[slot, 64:80, :].astype(F32)[0:1, tokens - 1:] == doc).astype(F32)
    seen[...] = jnp.broadcast_to(count, seen.shape)

    for k in range(1, n_z):
        @pl.when(z + k < n_z)
        def _(k=k):
            remote(z_tops.at[z + k], z_tops.at[z + k], z_send.at[k], z_recv.at[z + k], ctx, me).wait_recv()
    amax_out[...] = jnp.maximum(jnp.max(z_tops[...], axis=0), chain[1])
    qn_load.wait()

    for d in (1, 2, 3):
        spread_top(d).wait_send()
    for k in range(1, n_z):
        pl.when(z - k >= 0)(spread_z(k).wait_send)
    pl.when(z < n_z - 1)(step().wait_send)
    chunk3.wait_send()
    sent(own)
    earlier(sent)

    @pl.when(next2)
    def _():
        for copy in chunk1:
            copy.wait_send()
        keys2.wait_send()

    @pl.when(next3)
    def _():
        for copy in chunk0:
            copy.wait_send()
        keys3.wait_send()

    passed(own)
    passed(late)
    pl.when(has1)(keys_on[0][1].wait_send)

    @pl.when(core == 0)
    def _():
        keys_own.wait_send()


def attend(
    gain, seen, qn, qx, kt, kx, vals, oldest, uk, uv, amax, out, amax_out, kt0, vals0, outs, store, amax_store
):
    heads, hd, width = uk.shape
    tokens = qn.shape[0]
    write_amax = pltpu.make_async_copy(amax, amax_out, amax_store)
    write_amax.start()
    count = jnp.max(seen[...]).astype(jnp.int32)
    together = min(heads, 8)
    q_at = lax.broadcasted_iota(jnp.int32, (tokens, tokens), 0)
    k_at = lax.broadcasted_iota(jnp.int32, (tokens, tokens), 1)

    def write(p):
        some = pl.ds(pl.multiple_of(p * 4 * hd, 4 * hd), 4 * hd)
        return pltpu.make_async_copy(outs.at[:, some], out.at[:, some], store.at[p])

    @pl.when(count == 3)
    def _():
        def some(g, carry):
            c = oldest[...]
            up = nt(uk[pl.ds(4 * g, 4)].reshape(4 * hd, width), c) * gain
            kt0[pl.ds(4 * g, 4)] = up.astype(BF16).reshape(4, hd, tokens)
            for p in range(2):
                h = 4 * g + 2 * p
                both = nn(c, jnp.concatenate([uv[h], uv[h + 1]], axis=1)).astype(BF16)
                vals0[h] = both[:, :hd]
                vals0[h + 1] = both[:, hd:]
            return carry

        lax.fori_loop(0, heads // 4, some, 0)

    def with_blocks(blocks):
        past = blocks * tokens

        def group(g, carry):
            for i in range(together):
                h = together * g + i
                e = i % 2
                cols = pl.ds(pl.multiple_of(h * hd, hd), hd)
                q = jnp.concatenate([qn[:, cols], qx[h]], axis=1)
                if blocks == 3:
                    k = jnp.concatenate([kt0[h], kt[h]], axis=1)
                    v = jnp.concatenate([vals0[h], vals[h]], axis=0)
                else:
                    k = kt[h, :, (2 - blocks) * tokens:]
                    v = vals[h, (2 - blocks) * tokens:, :]
                k = jnp.concatenate([k, kx[e, :, (3 - blocks) * tokens:]], axis=0)
                s = nn(q, k)
                own = jnp.where(k_at <= q_at, s[:, past:], HIDDEN)
                s = jnp.concatenate([s[:, :past], own], axis=1) if blocks else own
                w = jnp.exp2(s - jnp.max(s, axis=1, keepdims=True)).astype(BF16)
                o = nn(w, jnp.concatenate([v, jnp.ones((past + tokens, hd), BF16)], axis=1))
                outs[:, cols] = (o[:, :hd] / o[:, hd:]).astype(BF16)
                if i % 4 == 3:
                    write(together // 4 * g + i // 4).start()
            return carry

        lax.fori_loop(0, heads // together, group, 0)

    for blocks in range(4):
        pl.when(count == blocks)(functools.partial(with_blocks, blocks))

    def written(p, carry):
        write(p).wait()
        return carry

    lax.fori_loop(0, heads // 4, written, 0)
    write_amax.wait()


def shards(n_ctx, n_head, q_nope, q_rope, latent, amax_prior, k_rope, w_uk, w_uv, seg_ids):
    tokens, columns = q_nope.shape
    heads, hd, width = w_uk.shape
    rope = k_rope.shape[0]
    rows = latent.shape[0]
    gain = math.log2(math.e) * (hd + rope) ** -0.5
    q_cos, q_sin, k_cos, k_sin = tables(tokens, rope, gain)
    n_z = n_ctx // 4
    keys = BLOCKS * tokens
    dma = pltpu.SemaphoreType.DMA
    anywhere = pl.BlockSpec(memory_space=pl.ANY)
    in_vmem = pl.BlockSpec(memory_space=pltpu.VMEM)
    mib = 1024 * 1024
    operands = (
        latent, amax_prior.reshape(1, width), k_rope, seg_ids.reshape(1, tokens), q_nope, q_rope, w_uk, w_uv,
        jnp.asarray(q_cos), jnp.asarray(q_sin), jnp.asarray(k_cos), jnp.asarray(k_sin),
    )
    results = pl.pallas_call(
        functools.partial(kernel, n_ctx, n_head, gain),
        out_shape=(
            pltpu.VMEM((8, 128), F32),
            pltpu.VMEM((tokens, columns), BF16),
            pltpu.VMEM((heads, tokens, 128), BF16),
            pltpu.VMEM((heads, hd, keys - tokens), BF16),
            pltpu.VMEM((2, 128, keys), BF16),
            pltpu.VMEM((heads, keys - tokens, hd), BF16),
            pltpu.VMEM((tokens, width), BF16),
            pltpu.VMEM((heads, hd, width), BF16),
            pltpu.VMEM((heads, width, hd), BF16),
            pltpu.VMEM((1, width), F32),
        ),
        in_specs=[pl.BlockSpec(memory_space=pltpu.HBM)] * 12,
        out_specs=(in_vmem,) * 10,
        scratch_shapes=[
            pltpu.VMEM((BLOCKS, tokens, width), BF16),
            pltpu.VMEM((BLOCKS, rope + 16, tokens), BF16),
            pltpu.VMEM((4, 1, width), F32),
            pltpu.VMEM((n_z, 1, width), F32),
            pltpu.VMEM((2, 1, width), F32),
            pltpu.VMEM((1, width), F32),
            pltpu.VMEM((1, tokens), jnp.int32),
            pltpu.VMEM((tokens, heads * rope), BF16),
            pltpu.VMEM(q_cos.shape, F32),
            pltpu.VMEM(q_sin.shape, F32),
            pltpu.VMEM(k_cos.shape, F32),
            pltpu.VMEM(k_sin.shape, F32),
            pltpu.VMEM((tokens, width), BF16),
            dma((BLOCKS, 2)),
            dma((BLOCKS, 2)),
            dma((BLOCKS, 2)),
            dma((BLOCKS, 2)),
            dma((BLOCKS, 2)),
            dma((BLOCKS, 2)),
            dma((BLOCKS,)),
            dma((BLOCKS,)),
            dma((2, 5)),
            dma((BLOCKS, 5)),
            dma((4,)),
            dma((4,)),
            dma((n_z,)),
            dma((n_z,)),
            dma,
            dma,
            dma((12,)),
        ],
        compiler_params=pltpu.CompilerParams(collective_id=0, has_side_effects=True, vmem_limit_bytes=16 * mib),
        cost_estimate=pl.CostEstimate(flops=4_000_000_000, bytes_accessed=8_000_000, transcendentals=0),
    )(*(pltpu.with_memory_space_constraint(x, pltpu.HBM) for x in operands))
    attended, latent_amax = pl.pallas_call(
        functools.partial(attend, gain),
        out_shape=(jax.ShapeDtypeStruct((tokens, columns), BF16), jax.ShapeDtypeStruct((1, width), F32)),
        in_specs=[in_vmem] * 10,
        out_specs=(anywhere, anywhere),
        scratch_shapes=[
            pltpu.VMEM((heads, hd, tokens), BF16),
            pltpu.VMEM((heads, tokens, hd), BF16),
            pltpu.VMEM((tokens, columns), BF16),
            dma((heads // 4,)),
            dma,
        ],
        compiler_params=pltpu.CompilerParams(vmem_limit_bytes=24 * mib),
        cost_estimate=pl.CostEstimate(flops=10_000_000_000, bytes_accessed=8_000_000, transcendentals=4_194_304),
    )(*(pltpu.with_memory_space_constraint(x, pltpu.VMEM) for x in results))
    return attended, latent_amax.reshape(width)


def solution(mesh):
    placed = (
        P("ctx", "head"),
        P("ctx", "head"),
        P(("ctx", "head"), None),
        P(),
        P(None, "ctx"),
        P("head", None, None),
        P("head", None, None),
        P("ctx"),
    )
    return jax.shard_map(
        functools.partial(shards, mesh.shape["ctx"], mesh.shape["head"]),
        mesh=mesh, in_specs=placed, out_specs=(P("ctx", "head"), P()), check_vma=False,
    )
```

```python
import functools
import math

import jax
import jax.numpy as jnp
import numpy as np
from jax import lax
from jax.experimental import pallas as pl
from jax.experimental.pallas import tpu as pltpu
from jax.sharding import PartitionSpec as P

MESH = pl.DeviceIdType.MESH
BF16 = jnp.bfloat16
F32 = jnp.float32
BLOCKS = 4
HIDDEN = -1e30


def tables(tokens, rope, gain):
    half = rope // 2
    freq = np.exp(np.arange(half) * (-2.0 * math.log(10000.0) / rope))
    q_angle = np.arange(tokens)[:, None] * freq[None, :]
    q_cos = np.tile(np.cos(q_angle), (1, 4)).astype(np.float32)
    q_sin = np.tile(np.sin(q_angle), (1, 4)).astype(np.float32)
    k_place = np.arange(BLOCKS * tokens) - (BLOCKS - 1) * tokens
    k_angle = freq[:, None] * k_place[None, :]
    k_cos = (np.cos(k_angle) * gain).astype(np.float32)
    k_sin = (np.sin(k_angle) * gain).astype(np.float32)
    return q_cos, q_sin, k_cos, k_sin


def nt(a, b):
    return lax.dot_general(a, b, (((1,), (1,)), ((), ())), preferred_element_type=F32)


def nn(a, b):
    return jnp.dot(a, b, preferred_element_type=F32)


def kernel(
    n_ctx, n_head, gain,
    latent, prior, k_rope, seg, q_nope, q_rope, w_uk, w_uv, q_cos, q_sin, k_cos, k_sin,
    seen, own_out, own_top, qn, qx, kt, kx, vals, oldest, uk, uv, amax_out,
    lat, tops, z_tops, prior_v, seg_v, qr, qc, qs, kc, ks, clipped, kt3, vals3,
    own_recv, own_send, pair_recv, pair_send, side_recv, side_send, far_recv, far_send,
    sib_send, sib_recv, tops_recv, tops_send, z_recv, z_send, load,
):
    ctx = lax.axis_index("ctx")
    me = lax.axis_index("head")
    core = lax.rem(ctx, 2)
    sibling = ctx + 1 - 2 * core
    n_z = n_ctx // 4
    z = ctx // 4
    heads, hd, width = uk.shape
    tokens = qn.shape[0]
    rope = k_rope.shape[0]
    rows = latent.shape[0]
    half = rope // 2
    mine = pl.ds(pl.multiple_of(me * rows, rows), rows)
    block = pl.ds(0, tokens)
    key_rows = pl.ds(tokens, half + 16)

    kind = lax.rem(ctx, 4)
    has1 = ctx >= 2
    has2 = (core == 1) | (ctx >= 2)
    has0 = ctx >= 3
    next2 = ctx + 2 < n_ctx
    next3 = (core == 1) & (ctx + 3 < n_ctx)

    beside = me + 1 - 2 * lax.rem(me, 2)
    up = lax.rem(me + 2, n_head)
    down = lax.rem(me + n_head - 2, n_head)

    def remote(src, dst, send, recv, c, h):
        return pltpu.make_async_remote_copy(
            src_ref=src, dst_ref=dst, send_sem=send, recv_sem=recv, device_id=(c, h), device_id_type=MESH
        )

    loads = [
        (latent, lat.at[3, mine]),
        (k_rope.at[pl.ds(0, half)], lat.at[3, pl.ds(tokens, half), pl.ds(0, tokens)]),
        (k_rope.at[pl.ds(half, half)], lat.at[3, pl.ds(tokens, half), pl.ds(tokens, tokens)]),
        (seg, seg_v), (prior, prior_v),
        (q_rope, qr), (q_cos, qc), (q_sin, qs), (k_cos, kc), (k_sin, ks), (w_uk, uk), (w_uv, uv), (q_nope, qn),
    ]
    loading = [pltpu.make_async_copy(src, dst, load.at[i]) for i, (src, dst) in enumerate(loads)]
    for copy in loading[:10]:
        copy.start()

    barrier = pltpu.get_barrier_semaphore()

    def greet(c, h):
        pl.semaphore_signal(barrier, inc=1, device_id=(c, h), device_id_type=MESH)

    @pl.when(has1)
    def _():
        greet(ctx - 2, me)
        greet(ctx - 2, beside)

    @pl.when((core == 0) & has0)
    def _():
        greet(ctx - 3, me)
        greet(ctx - 3, beside)

    for k in range(1, n_head):
        greet(ctx, lax.rem(me + k, n_head))
    for d in (1, 2, 3):
        greet(4 * z + lax.rem(kind + d, 4), me)
    for k in range(1, n_z):
        greet(4 * lax.rem(z + k, n_z) + kind, me)

    for slot, there in ((0, has0), (1, has1), (2, has2)):
        @pl.when(jnp.logical_not(there))
        def _(slot=slot):
            lat[slot, block, :] = jnp.zeros((tokens, width), BF16)
            lat[slot, key_rows, :] = jnp.full((half + 16, width), -1.0, BF16)

    for copy in loading[:4]:
        copy.wait()
    lat[3, pl.ds(tokens + half, 16), :] = jnp.broadcast_to(
        jnp.concatenate([seg_v[...], seg_v[...]], axis=1).astype(F32), (16, width)
    ).astype(BF16)
    listeners = 2 * (next2.astype(jnp.int32) + next3.astype(jnp.int32))
    pl.semaphore_wait(barrier, n_head - 1 + 3 + (n_z - 1) + listeners)

    def share(k):
        return remote(
            lat.at[3, mine], lat.at[3, mine], own_send, own_recv, ctx, lax.rem(me + k, n_head)
        )

    def chunk(slot, i, c, h):
        return remote(lat.at[3, mine], lat.at[slot, mine], pair_send.at[slot, i], pair_recv.at[slot, i], c, h)

    def keys_to(slot, c):
        return remote(lat.at[3, key_rows], lat.at[slot, key_rows], pair_send.at[slot, 2], pair_recv.at[slot, 2], c, me)

    ahead2 = [chunk(1, 0, ctx + 2, me), chunk(1, 1, ctx + 2, beside), keys_to(1, ctx + 2)]
    ahead3 = [chunk(0, 0, ctx + 3, me), chunk(0, 1, ctx + 3, beside), keys_to(0, ctx + 3)]

    @pl.when(next2)
    def _():
        for copy in ahead2:
            copy.start()

    for k in range(1, n_head):
        share(k).start()

    @pl.when(next3)
    def _():
        for copy in ahead3:
            copy.start()

    for copy in loading[10:]:
        copy.start()

    for copy in loading[4:10]:
        copy.wait()
    lane = lax.broadcasted_iota(jnp.int32, (tokens, 128), 1)
    docs = lax.broadcasted_iota(jnp.int32, (64, tokens), 0)
    docs = jnp.concatenate([docs, docs], axis=0)
    mark = (docs == jnp.broadcast_to(seg_v[...], (128, tokens))).astype(F32).T
    i = lax.broadcasted_iota(jnp.int32, (128, 128), 0)
    j = lax.broadcasted_iota(jnp.int32, (128, 128), 1)
    low = (j & 63) < 32
    swap = jnp.where(low & (i == j + 32), -1.0, jnp.where(jnp.logical_not(low) & (i == j - 32), 1.0, 0.0)).astype(BF16)
    cosine, sine = qc[...], qs[...]

    def turn(p, carry):
        raw = qr[:, pl.ds(pl.multiple_of(p * 128, 128), 128)]
        turned = raw.astype(F32) * cosine + nn(raw, swap) * sine
        qx[2 * p] = jnp.where(lane < 64, turned, mark).astype(BF16)
        qx[2 * p + 1] = jnp.where(lane < 64, mark, turned).astype(BF16)
        return carry

    lax.fori_loop(0, heads // 2, turn, 0, unroll=2)

    def pair_at(h):
        return pl.ds(pl.multiple_of(h // 2 * 2 * rows, 2 * rows), 2 * rows)

    def one_at(h, x):
        return pl.ds(pl.multiple_of((h // 2 * 2 + x) * rows, rows), rows)

    def side(slots, i, to):
        at = lat.at[slots, pair_at(me)]
        return remote(at, at, side_send.at[i], side_recv.at[i], ctx, to)

    def far(slots, i, h, to):
        at = lat.at[slots, one_at(h, i)]
        return remote(at, at, far_send.at[i], far_recv.at[i], ctx, to)

    def sides(slots):
        side(slots, 0, up).start()
        side(slots, 1, down).start()

    def fars(slots):
        side(slots, 0, up).wait_recv()
        far(slots, 0, down, up).start()
        side(slots, 1, down).wait_recv()
        far(slots, 1, up, down).start()

    def complete(slots):
        far(slots, 0, down, up).wait_recv()
        far(slots, 1, up, down).wait_recv()

    def sent(slots):
        for i in range(2):
            side(slots, i, up).wait_send()
            far(slots, i, up, up).wait_send()

    with_oldest = (core == 0) & has0
    without_oldest = has1 & jnp.logical_not(with_oldest)

    def earlier(act):
        pl.when(with_oldest)(functools.partial(act, pl.ds(0, 2)))
        pl.when(without_oldest)(functools.partial(act, pl.ds(1, 1)))

    @pl.when(has1)
    def _():
        for copy in ahead2:
            copy.wait_recv()

    @pl.when(with_oldest)
    def _():
        for copy in ahead3:
            copy.wait_recv()

    earlier(sides)

    others = lat.at[3, pl.ds(0, (n_head - 1) * rows)]
    remote(others, others, own_send, own_recv, ctx, me).wait_recv()
    pass_own = remote(lat.at[3], lat.at[2], sib_send.at[0], sib_recv.at[2], sibling, me)
    pl.when(core == 0)(pass_own.start)
    tops[kind] = jnp.max(jnp.abs(lat[3, block, :].astype(F32)), axis=0, keepdims=True)

    def spread_top(d):
        return remote(tops.at[kind], tops.at[kind], tops_send, tops_recv, 4 * z + lax.rem(kind + d, 4), me)

    for d in (1, 2, 3):
        spread_top(d).start()

    limit = prior_v[...].astype(BF16)
    for copy in loading[10:]:
        copy.wait()

    def project(slot):
        at = pl.ds((slot - 1) * tokens, tokens)
        clipped[...] = jnp.clip(lat[slot, block, :], -limit, limit)

        def some(g, carry):
            c = clipped[...]
            ups = (nt(uk[pl.ds(4 * g, 4)].reshape(4 * hd, width), c) * gain).astype(BF16).reshape(4, hd, tokens)
            if slot == 3:
                kt3[pl.ds(4 * g, 4)] = ups
            else:
                kt[pl.ds(4 * g, 4), :, at] = ups
            for p in range(2):
                h = 4 * g + 2 * p
                both = nn(c, jnp.concatenate([uv[h], uv[h + 1]], axis=1)).astype(BF16)
                for e in range(2):
                    if slot == 3:
                        vals3[h + e] = both[:, e * hd:(e + 1) * hd]
                    else:
                        vals[h + e, at, :] = both[:, e * hd:(e + 1) * hd]
            return carry

        lax.fori_loop(0, heads // 4, some, 0)

    def turn_keys(slot):
        at = pl.ds(slot * tokens, tokens)
        a = lat[slot, pl.ds(tokens, half), 0:tokens].astype(F32)
        b = lat[slot, pl.ds(tokens, half), tokens:2 * tokens].astype(F32)
        cosine, sine = kc[:, at], ks[:, at]
        turned = jnp.concatenate([a * cosine - b * sine, b * cosine + a * sine], axis=0).astype(BF16)
        doc = jnp.broadcast_to(lat[slot, pl.ds(tokens + half, 16), 0:tokens].astype(F32)[0:1, :], (64, tokens))
        number = lax.broadcasted_iota(jnp.int32, (64, tokens), 0).astype(F32)
        other = jnp.where(doc == number, 0.0, HIDDEN).astype(BF16)
        kx[0, 0:64, at] = turned
        kx[0, 64:128, at] = other
        kx[1, 0:64, at] = other
        kx[1, 64:128, at] = turned

    project(3)
    turn_keys(3)
    earlier(fars)

    q_at = lax.broadcasted_iota(jnp.int32, (tokens, tokens), 0)
    k_at = lax.broadcasted_iota(jnp.int32, (tokens, tokens), 1)

    def attend_own(first):
        for h in range(first, first + heads // 2):
            q = jnp.concatenate([qn[:, h * hd:(h + 1) * hd], qx[h]], axis=1)
            k = jnp.concatenate([kt3[h], kx[h % 2, :, 3 * tokens:]], axis=0)
            s = jnp.where(k_at <= q_at, nn(q, k), HIDDEN)
            top = jnp.max(s, axis=1, keepdims=True)
            w = jnp.exp2(s - top).astype(BF16)
            own_out[h] = nn(w, jnp.concatenate([vals3[h], jnp.ones((tokens, hd), BF16)], axis=1))
            own_top[h] = jnp.broadcast_to(top, (tokens, hd))

    attend_own(0)

    three = tops.at[pl.ds(0, 3)]
    remote(three, three, tops_send, tops_recv, ctx, me).wait_recv()
    z_tops[z] = jnp.max(tops[...], axis=0)

    def spread_z(k):
        return remote(z_tops.at[z], z_tops.at[z], z_send, z_recv, 4 * lax.rem(z + k, n_z) + kind, me)

    for k in range(1, n_z):
        spread_z(k).start()

    earlier(complete)
    on = [
        ((core == 0) & has1, remote(lat.at[1], lat.at[0], sib_send.at[1], sib_recv.at[0], sibling, me)),
        ((core == 1) & has1, remote(lat.at[1], lat.at[2], sib_send.at[1], sib_recv.at[2], sibling, me)),
    ]
    for there, copy in on:
        pl.when(there)(copy.start)

    attend_own(heads // 2)
    project(1)
    turn_keys(1)

    pl.when(has2)(pass_own.wait_recv)
    project(2)
    turn_keys(2)

    pl.when((core == 1) & has0)(on[0][1].wait_recv)
    oldest[...] = jnp.clip(lat[0, block, :], -limit, limit)
    turn_keys(0)

    doc_at = pl.ds(tokens + half, 16)
    doc = lat[3, doc_at, 0:tokens].astype(F32)[0:1, 0:1]
    count = jnp.zeros((1, 1), F32)
    for slot in range(3):
        count += (lat[slot, doc_at, 0:tokens].astype(F32)[0:1, tokens - 1:] == doc).astype(F32)
    seen[...] = jnp.broadcast_to(count, seen.shape)

    rest = z_tops.at[pl.ds(0, n_z - 1)]
    remote(rest, rest, z_send, z_recv, ctx, me).wait_recv()
    amax_out[...] = jnp.max(z_tops[...], axis=0)

    remote(others, others, own_send, own_recv, ctx, me).wait_send()
    remote(three, three, tops_send, tops_recv, ctx, me).wait_send()
    remote(rest, rest, z_send, z_recv, ctx, me).wait_send()
    earlier(sent)

    @pl.when(next2)
    def _():
        for copy in ahead2:
            copy.wait_send()

    @pl.when(next3)
    def _():
        for copy in ahead3:
            copy.wait_send()

    pl.when(core == 0)(pass_own.wait_send)
    pl.when(has1)(on[0][1].wait_send)


def attend(
    gain, seen, own_out, own_top, qn, qx, kt, kx, vals, oldest, uk, uv, amax,
    out, amax_out, kt0, vals0, outs, store, amax_store,
):
    heads, hd, width = uk.shape
    tokens = qn.shape[0]
    write_amax = pltpu.make_async_copy(amax, amax_out, amax_store)
    write_amax.start()
    count = jnp.max(seen[...]).astype(jnp.int32)
    together = min(heads, 8)

    def write(p):
        some = pl.ds(pl.multiple_of(p * 4 * hd, 4 * hd), 4 * hd)
        return pltpu.make_async_copy(outs.at[:, some], out.at[:, some], store.at[p])

    @pl.when(count == 3)
    def _():
        def some(g, carry):
            c = oldest[...]
            ups = nt(uk[pl.ds(4 * g, 4)].reshape(4 * hd, width), c) * gain
            kt0[pl.ds(4 * g, 4)] = ups.astype(BF16).reshape(4, hd, tokens)
            for p in range(2):
                h = 4 * g + 2 * p
                both = nn(c, jnp.concatenate([uv[h], uv[h + 1]], axis=1)).astype(BF16)
                vals0[h] = both[:, :hd]
                vals0[h + 1] = both[:, hd:]
            return carry

        lax.fori_loop(0, heads // 4, some, 0)

    def with_blocks(blocks):
        def group(g, carry):
            for i in range(together):
                h = together * g + i
                e = i % 2
                cols = pl.ds(pl.multiple_of(h * hd, hd), hd)
                o = own_out[h]
                if blocks:
                    q = jnp.concatenate([qn[:, cols], qx[h]], axis=1)
                    if blocks == 3:
                        k = jnp.concatenate([kt0[h], kt[h]], axis=1)
                        v = jnp.concatenate([vals0[h], vals[h]], axis=0)
                    else:
                        k = kt[h, :, (2 - blocks) * tokens:]
                        v = vals[h, (2 - blocks) * tokens:, :]
                    k = jnp.concatenate([k, kx[e, :, (3 - blocks) * tokens:3 * tokens]], axis=0)
                    s = nn(q, k)
                    own = own_top[h]
                    top = jnp.maximum(jnp.max(s, axis=1, keepdims=True), own[:, 0:1])
                    w = jnp.exp2(s - top).astype(BF16)
                    scale = jnp.exp2(own - top)
                    o = o * jnp.concatenate([scale, scale], axis=1) + nn(
                        w, jnp.concatenate([v, jnp.ones((blocks * tokens, hd), BF16)], axis=1)
                    )
                outs[:, cols] = (o[:, :hd] / o[:, hd:]).astype(BF16)
                if i % 4 == 3:
                    write(together // 4 * g + i // 4).start()
            return carry

        lax.fori_loop(0, heads // together, group, 0)

    for blocks in range(4):
        pl.when(count == blocks)(functools.partial(with_blocks, blocks))

    def written(p, carry):
        write(p).wait()
        return carry

    lax.fori_loop(0, heads // 4, written, 0)
    write_amax.wait()


def shards(n_ctx, n_head, q_nope, q_rope, latent, amax_prior, k_rope, w_uk, w_uv, seg_ids):
    tokens, columns = q_nope.shape
    heads, hd, width = w_uk.shape
    rope = k_rope.shape[0]
    rows = latent.shape[0]
    gain = math.log2(math.e) * (hd + rope) ** -0.5
    q_cos, q_sin, k_cos, k_sin = tables(tokens, rope, gain)
    n_z = n_ctx // 4
    keys = BLOCKS * tokens
    dma = pltpu.SemaphoreType.DMA
    anywhere = pl.BlockSpec(memory_space=pl.ANY)
    in_vmem = pl.BlockSpec(memory_space=pltpu.VMEM)
    mib = 1024 * 1024
    operands = (
        latent, amax_prior.reshape(1, width), k_rope, seg_ids.reshape(1, tokens), q_nope, q_rope, w_uk, w_uv,
        jnp.asarray(q_cos), jnp.asarray(q_sin), jnp.asarray(k_cos), jnp.asarray(k_sin),
    )
    results = pl.pallas_call(
        functools.partial(kernel, n_ctx, n_head, gain),
        out_shape=(
            pltpu.VMEM((8, 128), F32),
            pltpu.VMEM((heads, tokens, 2 * hd), F32),
            pltpu.VMEM((heads, tokens, hd), F32),
            pltpu.VMEM((tokens, columns), BF16),
            pltpu.VMEM((heads, tokens, 128), BF16),
            pltpu.VMEM((heads, hd, 2 * tokens), BF16),
            pltpu.VMEM((2, 128, keys), BF16),
            pltpu.VMEM((heads, 2 * tokens, hd), BF16),
            pltpu.VMEM((tokens, width), BF16),
            pltpu.VMEM((heads, hd, width), BF16),
            pltpu.VMEM((heads, width, hd), BF16),
            pltpu.VMEM((1, width), F32),
        ),
        in_specs=[pl.BlockSpec(memory_space=pltpu.HBM)] * 12,
        out_specs=(in_vmem,) * 12,
        scratch_shapes=[
            pltpu.VMEM((BLOCKS, tokens + rope // 2 + 16, width), BF16),
            pltpu.VMEM((4, 1, width), F32),
            pltpu.VMEM((n_z, 1, width), F32),
            pltpu.VMEM((1, width), F32),
            pltpu.VMEM((1, tokens), jnp.int32),
            pltpu.VMEM((tokens, heads * rope), BF16),
            pltpu.VMEM(q_cos.shape, F32),
            pltpu.VMEM(q_sin.shape, F32),
            pltpu.VMEM(k_cos.shape, F32),
            pltpu.VMEM(k_sin.shape, F32),
            pltpu.VMEM((tokens, width), BF16),
            pltpu.VMEM((heads, hd, tokens), BF16),
            pltpu.VMEM((heads, tokens, hd), BF16),
            dma,
            dma,
            dma((2, 3)),
            dma((2, 3)),
            dma((2,)),
            dma((2,)),
            dma((2,)),
            dma((2,)),
            dma((2,)),
            dma((BLOCKS,)),
            dma,
            dma,
            dma,
            dma,
            dma((13,)),
        ],
        compiler_params=pltpu.CompilerParams(collective_id=0, has_side_effects=True, vmem_limit_bytes=18 * mib),
        cost_estimate=pl.CostEstimate(flops=4_000_000_000, bytes_accessed=8_000_000, transcendentals=0),
    )(*(pltpu.with_memory_space_constraint(x, pltpu.HBM) for x in operands))
    attended, latent_amax = pl.pallas_call(
        functools.partial(attend, gain),
        out_shape=(jax.ShapeDtypeStruct((tokens, columns), BF16), jax.ShapeDtypeStruct((1, width), F32)),
        in_specs=[in_vmem] * 12,
        out_specs=(anywhere, anywhere),
        scratch_shapes=[
            pltpu.VMEM((heads, hd, tokens), BF16),
            pltpu.VMEM((heads, tokens, hd), BF16),
            pltpu.VMEM((tokens, columns), BF16),
            dma((heads // 4,)),
            dma,
        ],
        compiler_params=pltpu.CompilerParams(vmem_limit_bytes=18 * mib),
        cost_estimate=pl.CostEstimate(flops=10_000_000_000, bytes_accessed=8_000_000, transcendentals=4_194_304),
    )(*(pltpu.with_memory_space_constraint(x, pltpu.VMEM) for x in results))
    return attended, latent_amax.reshape(width)


def solution(mesh):
    placed = (
        P("ctx", "head"),
        P("ctx", "head"),
        P(("ctx", "head"), None),
        P(),
        P(None, "ctx"),
        P("head", None, None),
        P("head", None, None),
        P("ctx"),
    )
    return jax.shard_map(
        functools.partial(shards, mesh.shape["ctx"], mesh.shape["head"]),
        mesh=mesh, in_specs=placed, out_specs=(P("ctx", "head"), P()), check_vma=False,
    )
```

```python
import functools
import math

import jax
import jax.numpy as jnp
import numpy as np
from jax import lax
from jax.experimental import pallas as pl
from jax.experimental.pallas import tpu as pltpu
from jax.sharding import PartitionSpec as P

MESH = pl.DeviceIdType.MESH
BF16 = jnp.bfloat16
F32 = jnp.float32
BLOCKS = 4
HIDDEN = -1e30


def tables(tokens, rope, gain):
    half = rope // 2
    freq = np.exp(np.arange(half) * (-2.0 * math.log(10000.0) / rope))
    q_angle = np.arange(tokens)[:, None] * freq[None, :]
    q_cos = np.tile(np.cos(q_angle), (1, 4)).astype(np.float32)
    q_sin = np.tile(np.sin(q_angle), (1, 4)).astype(np.float32)
    k_place = np.arange(BLOCKS * tokens) - (BLOCKS - 1) * tokens
    k_angle = freq[:, None] * k_place[None, :]
    k_cos = (np.cos(k_angle) * gain).astype(np.float32)
    k_sin = (np.sin(k_angle) * gain).astype(np.float32)
    return q_cos, q_sin, k_cos, k_sin


def nt(a, b):
    return lax.dot_general(a, b, (((1,), (1,)), ((), ())), preferred_element_type=F32)


def nn(a, b):
    return jnp.dot(a, b, preferred_element_type=F32)


def kernel(
    n_ctx, n_head, gain,
    latent, prior, k_rope, seg, q_nope, q_rope, w_uk, w_uv, q_cos, q_sin, k_cos, k_sin,
    seen, own_out, own_top, qn, qx, kt, kx, vals, earlier_two, uk, uv, amax_out,
    lat, tops, z_tops, prior_v, seg_v, qr, qc, qs, kc, ks, clipped, kt3, vals3,
    own_recv, own_send, pair_recv, pair_send, side_recv, side_send, far_recv, far_send,
    sib_send, sib_recv, tops_recv, tops_send, z_recv, z_send, hello, load,
):
    ctx = lax.axis_index("ctx")
    me = lax.axis_index("head")
    core = lax.rem(ctx, 2)
    sibling = ctx + 1 - 2 * core
    n_z = n_ctx // 4
    z = ctx // 4
    heads, hd, width = uk.shape
    tokens = qn.shape[0]
    rope = k_rope.shape[0]
    rows = latent.shape[0]
    half = rope // 2
    mine = pl.ds(pl.multiple_of(me * rows, rows), rows)
    block = pl.ds(0, tokens)
    key_rows = pl.ds(tokens, half + 16)

    kind = lax.rem(ctx, 4)
    has1 = ctx >= 2
    has2 = (core == 1) | (ctx >= 2)
    has0 = ctx >= 3
    next2 = ctx + 2 < n_ctx
    next3 = (core == 1) & (ctx + 3 < n_ctx)

    beside = me + 1 - 2 * lax.rem(me, 2)
    up = lax.rem(me + 2, n_head)
    down = lax.rem(me + n_head - 2, n_head)

    def remote(src, dst, send, recv, c, h):
        return pltpu.make_async_remote_copy(
            src_ref=src, dst_ref=dst, send_sem=send, recv_sem=recv, device_id=(c, h), device_id_type=MESH
        )

    loads = [
        (latent, lat.at[3, mine]),
        (k_rope.at[pl.ds(0, half)], lat.at[3, pl.ds(tokens, half), pl.ds(0, tokens)]),
        (k_rope.at[pl.ds(half, half)], lat.at[3, pl.ds(tokens, half), pl.ds(tokens, tokens)]),
        (seg, seg_v), (prior, prior_v),
        (q_rope, qr), (q_cos, qc), (q_sin, qs), (k_cos, kc), (k_sin, ks), (w_uk, uk), (w_uv, uv), (q_nope, qn),
    ]
    loading = [pltpu.make_async_copy(src, dst, load.at[i]) for i, (src, dst) in enumerate(loads)]
    for copy in loading[:10]:
        copy.start()

    barrier = pltpu.get_barrier_semaphore()

    def greet(c, h):
        pl.semaphore_signal(barrier, inc=1, device_id=(c, h), device_id_type=MESH)

    @pl.when(has1)
    def _():
        greet(ctx - 2, me)
        greet(ctx - 2, beside)

    @pl.when((core == 0) & has0)
    def _():
        greet(ctx - 3, me)

    for k in range(1, n_head):
        greet(ctx, lax.rem(me + k, n_head))
    for d in (1, 2, 3):
        greet(4 * z + lax.rem(kind + d, 4), me)
    for k in range(1, n_z):
        pl.when(z + k < n_z)(functools.partial(greet, ctx + 4 * k, me))

    for slot, there in ((0, has0), (1, has1), (2, has2)):
        @pl.when(jnp.logical_not(there))
        def _(slot=slot):
            lat[slot, block, :] = jnp.zeros((tokens, width), BF16)
            lat[slot, key_rows, :] = jnp.full((half + 16, width), -1.0, BF16)

    for copy in loading[:4]:
        copy.wait()
    lat[3, pl.ds(tokens + half, 16), :] = jnp.broadcast_to(
        jnp.concatenate([seg_v[...], seg_v[...]], axis=1).astype(F32), (16, width)
    ).astype(BF16)
    listeners = 2 * next2.astype(jnp.int32) + next3.astype(jnp.int32)
    pl.semaphore_wait(barrier, n_head - 1 + 3 + z + listeners)

    def share(k):
        return remote(
            lat.at[3, mine], lat.at[3, mine], own_send, own_recv, ctx, lax.rem(me + k, n_head)
        )

    def chunk(slot, i, c, h):
        return remote(lat.at[3, mine], lat.at[slot, mine], pair_send.at[slot, i], pair_recv.at[slot, i], c, h)

    def keys_to(slot, c):
        return remote(lat.at[3, key_rows], lat.at[slot, key_rows], pair_send.at[slot, 2], pair_recv.at[slot, 2], c, me)

    ahead2 = [chunk(1, 0, ctx + 2, me), chunk(1, 1, ctx + 2, beside), keys_to(1, ctx + 2)]
    ahead3 = remote(lat.at[3], lat.at[0], sib_send.at[2], sib_recv.at[0], ctx + 3, me)

    @pl.when(next2)
    def _():
        for copy in ahead2:
            copy.start()

    for k in range(1, n_head):
        share(k).start()

    for copy in loading[10:]:
        copy.start()

    for k in range(1, n_z):
        @pl.when(z - k >= 0)
        def _(k=k):
            pl.semaphore_signal(hello, inc=1, device_id=(ctx - 4 * k, me), device_id_type=MESH)

    for copy in loading[4:10]:
        copy.wait()
    lane = lax.broadcasted_iota(jnp.int32, (tokens, 128), 1)
    docs = lax.broadcasted_iota(jnp.int32, (64, tokens), 0)
    docs = jnp.concatenate([docs, docs], axis=0)
    mark = (docs == jnp.broadcast_to(seg_v[...], (128, tokens))).astype(F32).T
    i = lax.broadcasted_iota(jnp.int32, (128, 128), 0)
    j = lax.broadcasted_iota(jnp.int32, (128, 128), 1)
    low = (j & 63) < 32
    swap = jnp.where(low & (i == j + 32), -1.0, jnp.where(jnp.logical_not(low) & (i == j - 32), 1.0, 0.0)).astype(BF16)
    cosine, sine = qc[...], qs[...]

    def turn(p, carry):
        raw = qr[:, pl.ds(pl.multiple_of(p * 128, 128), 128)]
        turned = raw.astype(F32) * cosine + nn(raw, swap) * sine
        qx[2 * p] = jnp.where(lane < 64, turned, mark).astype(BF16)
        qx[2 * p + 1] = jnp.where(lane < 64, mark, turned).astype(BF16)
        return carry

    lax.fori_loop(0, heads // 2, turn, 0, unroll=2)

    def pair_at(h):
        return pl.ds(pl.multiple_of(h // 2 * 2 * rows, 2 * rows), 2 * rows)

    def one_at(h, x):
        return pl.ds(pl.multiple_of((h // 2 * 2 + x) * rows, rows), rows)

    def side(slots, i, to):
        at = lat.at[slots, pair_at(me)]
        return remote(at, at, side_send.at[i], side_recv.at[i], ctx, to)

    def far(slots, i, h, to):
        at = lat.at[slots, one_at(h, i)]
        return remote(at, at, far_send.at[i], far_recv.at[i], ctx, to)

    def sides(slots):
        side(slots, 0, up).start()
        side(slots, 1, down).start()

    def fars(slots):
        side(slots, 0, up).wait_recv()
        far(slots, 0, down, up).start()
        side(slots, 1, down).wait_recv()
        far(slots, 1, up, down).start()

    def complete(slots):
        far(slots, 0, down, up).wait_recv()
        far(slots, 1, up, down).wait_recv()

    def sent(slots):
        for i in range(2):
            side(slots, i, up).wait_send()
            far(slots, i, up, up).wait_send()

    late = pl.ds(1, 1)

    def earlier(act):
        pl.when(has1)(functools.partial(act, late))

    @pl.when(has1)
    def _():
        for copy in ahead2:
            copy.wait_recv()

    earlier(sides)

    others = lat.at[3, pl.ds(0, (n_head - 1) * rows)]
    remote(others, others, own_send, own_recv, ctx, me).wait_recv()
    pass_own = remote(lat.at[3], lat.at[2], sib_send.at[0], sib_recv.at[2], sibling, me)
    pl.when(core == 0)(pass_own.start)
    pl.when(next3)(ahead3.start)
    tops[kind] = jnp.max(jnp.abs(lat[3, block, :].astype(F32)), axis=0, keepdims=True)

    def spread_top(d):
        return remote(tops.at[kind], tops.at[kind], tops_send, tops_recv, 4 * z + lax.rem(kind + d, 4), me)

    for d in (1, 2, 3):
        spread_top(d).start()

    limit = prior_v[...].astype(BF16)
    for copy in loading[10:]:
        copy.wait()

    def project(slot):
        kt_to, vals_to = (kt3, vals3) if slot == 3 else (kt, vals)
        clipped[...] = jnp.clip(lat[slot, block, :], -limit, limit)

        def some(g, carry):
            c = clipped[...]
            ups = (nt(uk[pl.ds(4 * g, 4)].reshape(4 * hd, width), c) * gain).astype(BF16).reshape(4, hd, tokens)
            kt_to[pl.ds(4 * g, 4)] = ups
            for p in range(2):
                h = 4 * g + 2 * p
                both = nn(c, jnp.concatenate([uv[h], uv[h + 1]], axis=1)).astype(BF16)
                for e in range(2):
                    vals_to[h + e] = both[:, e * hd:(e + 1) * hd]
            return carry

        lax.fori_loop(0, heads // 4, some, 0)

    def turn_keys(slot):
        at = pl.ds(slot * tokens, tokens)
        a = lat[slot, pl.ds(tokens, half), 0:tokens].astype(F32)
        b = lat[slot, pl.ds(tokens, half), tokens:2 * tokens].astype(F32)
        cosine, sine = kc[:, at], ks[:, at]
        turned = jnp.concatenate([a * cosine - b * sine, b * cosine + a * sine], axis=0).astype(BF16)
        doc = jnp.broadcast_to(lat[slot, pl.ds(tokens + half, 16), 0:tokens].astype(F32)[0:1, :], (64, tokens))
        number = lax.broadcasted_iota(jnp.int32, (64, tokens), 0).astype(F32)
        other = jnp.where(doc == number, 0.0, HIDDEN).astype(BF16)
        kx[0, 0:64, at] = turned
        kx[0, 64:128, at] = other
        kx[1, 0:64, at] = other
        kx[1, 64:128, at] = turned

    project(3)

    three = tops.at[pl.ds(0, 3)]
    remote(three, three, tops_send, tops_recv, ctx, me).wait_recv()
    z_tops[z] = jnp.max(tops[...], axis=0)
    pl.when(z < n_z - 1)(lambda: pl.semaphore_wait(hello, n_z - 1 - z))

    def spread_z(k):
        return remote(z_tops.at[z], z_tops.at[z], z_send, z_recv, 4 * lax.rem(z + k, n_z) + kind, me)

    for k in range(1, n_z):
        spread_z(k).start()

    turn_keys(3)
    earlier(fars)

    q_at = lax.broadcasted_iota(jnp.int32, (tokens, tokens), 0)
    k_at = lax.broadcasted_iota(jnp.int32, (tokens, tokens), 1)

    def attend_own(first):
        for h in range(first, first + heads // 2):
            q = jnp.concatenate([qn[:, h * hd:(h + 1) * hd], qx[h]], axis=1)
            k = jnp.concatenate([kt3[h], kx[h % 2, :, 3 * tokens:]], axis=0)
            s = jnp.where(k_at <= q_at, nn(q, k), HIDDEN)
            top = jnp.max(s, axis=1, keepdims=True)
            w = jnp.exp2(s - top).astype(BF16)
            own_out[h] = nn(w, jnp.concatenate([vals3[h], jnp.ones((tokens, hd), BF16)], axis=1))
            own_top[h] = jnp.broadcast_to(top, (tokens, hd))

    attend_own(0)

    earlier(complete)
    on = [
        ((core == 0) & has1, remote(lat.at[1], lat.at[0], sib_send.at[1], sib_recv.at[0], sibling, me)),
        ((core == 1) & has1, remote(lat.at[1], lat.at[2], sib_send.at[1], sib_recv.at[2], sibling, me)),
    ]
    for there, copy in on:
        pl.when(there)(copy.start)

    attend_own(heads // 2)
    earlier_two[1] = jnp.clip(lat[1, block, :], -limit, limit)
    turn_keys(1)

    pl.when(has2)(pass_own.wait_recv)
    project(2)
    turn_keys(2)

    pl.when(has0)(ahead3.wait_recv)
    earlier_two[0] = jnp.clip(lat[0, block, :], -limit, limit)
    turn_keys(0)

    doc_at = pl.ds(tokens + half, 16)
    doc = lat[3, doc_at, 0:tokens].astype(F32)[0:1, 0:1]
    count = jnp.zeros((1, 1), F32)
    for slot in range(3):
        count += (lat[slot, doc_at, 0:tokens].astype(F32)[0:1, tokens - 1:] == doc).astype(F32)
    wide = (lat[3, doc_at, 0:tokens].astype(F32)[0:1, tokens // 2:tokens // 2 + 1] == doc).astype(F32)
    seen[...] = jnp.broadcast_to(count + 4.0 * wide, seen.shape)

    rest = z_tops.at[pl.ds(0, n_z - 1)]
    remote(rest, rest, z_send, z_recv, ctx, me).wait_recv()
    amax_out[...] = jnp.max(z_tops[...], axis=0)

    remote(others, others, own_send, own_recv, ctx, me).wait_send()
    remote(three, three, tops_send, tops_recv, ctx, me).wait_send()
    remote(rest, rest, z_send, z_recv, ctx, me).wait_send()
    earlier(sent)

    @pl.when(next2)
    def _():
        for copy in ahead2:
            copy.wait_send()

    pl.when(next3)(ahead3.wait_send)
    pl.when(core == 0)(pass_own.wait_send)
    pl.when(has1)(on[0][1].wait_send)


def attend(
    gain, seen, own_out, own_top, qn, qx, kt, kx, vals, earlier_two, uk, uv, amax,
    out, amax_out, kt_two, vals_two, outs, store, amax_store,
):
    heads, hd, width = uk.shape
    tokens = qn.shape[0]
    write_amax = pltpu.make_async_copy(amax, amax_out, amax_store)
    write_amax.start()
    code = jnp.max(seen[...]).astype(jnp.int32)
    count = code & 3
    middle = tokens // 2
    together = min(heads, 8)

    def write(p):
        some = pl.ds(pl.multiple_of(p * 4 * hd, 4 * hd), 4 * hd)
        return pltpu.make_async_copy(outs.at[:, some], out.at[:, some], store.at[p])

    for slot in range(2):
        @pl.when(count >= 3 - slot)
        def _(slot=slot):
            def some(g, carry):
                c = earlier_two[slot]
                ups = nt(uk[pl.ds(4 * g, 4)].reshape(4 * hd, width), c) * gain
                kt_two[slot, pl.ds(4 * g, 4)] = ups.astype(BF16).reshape(4, hd, tokens)
                for p in range(2):
                    h = 4 * g + 2 * p
                    both = nn(c, jnp.concatenate([uv[h], uv[h + 1]], axis=1)).astype(BF16)
                    vals_two[slot, h] = both[:, :hd]
                    vals_two[slot, h + 1] = both[:, hd:]
                return carry

            lax.fori_loop(0, heads // 4, some, 0)

    def with_blocks(blocks, wide):
        seeing = 0 if not blocks else tokens if wide else middle
        skip = middle if wide and blocks == 3 else 0

        def group(g, carry):
            for i in range(together):
                h = together * g + i
                e = i % 2
                cols = pl.ds(pl.multiple_of(h * hd, hd), hd)
                if blocks:
                    q = jnp.concatenate([qn[0:seeing, cols], qx[h, 0:seeing, :]], axis=1)
                    k = [kt_two[x, h] for x in range(3 - blocks, 2)] + [kt[h]]
                    v = [vals_two[x, h] for x in range(3 - blocks, 2)] + [vals[h]]
                    k[0], v[0] = k[0][:, skip:], v[0][skip:]
                    k = jnp.concatenate(k, axis=1)
                    v = jnp.concatenate(v, axis=0)
                    k = jnp.concatenate([k, kx[e, :, (3 - blocks) * tokens + skip:3 * tokens]], axis=0)
                    s = nn(q, k)
                    own = own_top[h, 0:seeing, :]
                    top = jnp.maximum(jnp.broadcast_to(jnp.max(s, axis=1, keepdims=True), own.shape), own)
                    w = jnp.exp2(s - jnp.concatenate([top] * (s.shape[1] // hd), axis=1)).astype(BF16)
                    scale = jnp.exp2(own - top)
                    o = own_out[h, 0:seeing, :] * jnp.concatenate([scale, scale], axis=1) + nn(
                        w, jnp.concatenate([v, jnp.ones(v.shape, BF16)], axis=1)
                    )
                    outs[0:seeing, cols] = (o[:, :hd] / o[:, hd:]).astype(BF16)
                if seeing < tokens:
                    o = own_out[h, seeing:, :]
                    outs[seeing:, cols] = (o[:, :hd] / o[:, hd:]).astype(BF16)
                if i % 4 == 3:
                    write(together // 4 * g + i // 4).start()
            return carry

        lax.fori_loop(0, heads // together, group, 0)

    pl.when(count == 0)(functools.partial(with_blocks, 0, False))
    for blocks in range(1, 4):
        for wide in (False, True):
            pl.when(code == blocks + 4 * wide)(functools.partial(with_blocks, blocks, wide))

    def written(p, carry):
        write(p).wait()
        return carry

    lax.fori_loop(0, heads // 4, written, 0)
    write_amax.wait()


def shards(n_ctx, n_head, q_nope, q_rope, latent, amax_prior, k_rope, w_uk, w_uv, seg_ids):
    tokens, columns = q_nope.shape
    heads, hd, width = w_uk.shape
    rope = k_rope.shape[0]
    rows = latent.shape[0]
    gain = math.log2(math.e) * (hd + rope) ** -0.5
    q_cos, q_sin, k_cos, k_sin = tables(tokens, rope, gain)
    n_z = n_ctx // 4
    keys = BLOCKS * tokens
    dma = pltpu.SemaphoreType.DMA
    anywhere = pl.BlockSpec(memory_space=pl.ANY)
    in_vmem = pl.BlockSpec(memory_space=pltpu.VMEM)
    mib = 1024 * 1024
    operands = (
        latent, amax_prior.reshape(1, width), k_rope, seg_ids.reshape(1, tokens), q_nope, q_rope, w_uk, w_uv,
        jnp.asarray(q_cos), jnp.asarray(q_sin), jnp.asarray(k_cos), jnp.asarray(k_sin),
    )
    results = pl.pallas_call(
        functools.partial(kernel, n_ctx, n_head, gain),
        out_shape=(
            pltpu.VMEM((8, 128), F32),
            pltpu.VMEM((heads, tokens, 2 * hd), F32),
            pltpu.VMEM((heads, tokens, hd), F32),
            pltpu.VMEM((tokens, columns), BF16),
            pltpu.VMEM((heads, tokens, 128), BF16),
            pltpu.VMEM((heads, hd, tokens), BF16),
            pltpu.VMEM((2, 128, keys), BF16),
            pltpu.VMEM((heads, tokens, hd), BF16),
            pltpu.VMEM((2, tokens, width), BF16),
            pltpu.VMEM((heads, hd, width), BF16),
            pltpu.VMEM((heads, width, hd), BF16),
            pltpu.VMEM((1, width), F32),
        ),
        in_specs=[pl.BlockSpec(memory_space=pltpu.HBM)] * 12,
        out_specs=(in_vmem,) * 12,
        scratch_shapes=[
            pltpu.VMEM((BLOCKS, tokens + rope // 2 + 16, width), BF16),
            pltpu.VMEM((4, 1, width), F32),
            pltpu.VMEM((n_z, 1, width), F32),
            pltpu.VMEM((1, width), F32),
            pltpu.VMEM((1, tokens), jnp.int32),
            pltpu.VMEM((tokens, heads * rope), BF16),
            pltpu.VMEM(q_cos.shape, F32),
            pltpu.VMEM(q_sin.shape, F32),
            pltpu.VMEM(k_cos.shape, F32),
            pltpu.VMEM(k_sin.shape, F32),
            pltpu.VMEM((tokens, width), BF16),
            pltpu.VMEM((heads, hd, tokens), BF16),
            pltpu.VMEM((heads, tokens, hd), BF16),
            dma,
            dma,
            dma((2, 3)),
            dma((2, 3)),
            dma((2,)),
            dma((2,)),
            dma((2,)),
            dma((2,)),
            dma((3,)),
            dma((BLOCKS,)),
            dma,
            dma,
            dma,
            dma,
            pltpu.SemaphoreType.REGULAR,
            dma((13,)),
        ],
        compiler_params=pltpu.CompilerParams(collective_id=0, has_side_effects=True, vmem_limit_bytes=18 * mib),
        cost_estimate=pl.CostEstimate(flops=4_000_000_000, bytes_accessed=8_000_000, transcendentals=0),
    )(*(pltpu.with_memory_space_constraint(x, pltpu.HBM) for x in operands))
    attended, latent_amax = pl.pallas_call(
        functools.partial(attend, gain),
        out_shape=(jax.ShapeDtypeStruct((tokens, columns), BF16), jax.ShapeDtypeStruct((1, width), F32)),
        in_specs=[in_vmem] * 12,
        out_specs=(anywhere, anywhere),
        scratch_shapes=[
            pltpu.VMEM((2, heads, hd, tokens), BF16),
            pltpu.VMEM((2, heads, tokens, hd), BF16),
            pltpu.VMEM((tokens, columns), BF16),
            dma((heads // 4,)),
            dma,
        ],
        compiler_params=pltpu.CompilerParams(vmem_limit_bytes=18 * mib),
        cost_estimate=pl.CostEstimate(flops=10_000_000_000, bytes_accessed=8_000_000, transcendentals=4_194_304),
    )(*(pltpu.with_memory_space_constraint(x, pltpu.VMEM) for x in results))
    return attended, latent_amax.reshape(width)


def solution(mesh):
    placed = (
        P("ctx", "head"),
        P("ctx", "head"),
        P(("ctx", "head"), None),
        P(),
        P(None, "ctx"),
        P("head", None, None),
        P("head", None, None),
        P("ctx"),
    )
    return jax.shard_map(
        functools.partial(shards, mesh.shape["ctx"], mesh.shape["head"]),
        mesh=mesh, in_specs=placed, out_specs=(P("ctx", "head"), P()), check_vma=False,
    )
```

```python
import functools
import math

import jax
import jax.numpy as jnp
import numpy as np
from jax import lax
from jax.experimental import pallas as pl
from jax.experimental.pallas import tpu as pltpu
from jax.sharding import PartitionSpec as P

MESH = pl.DeviceIdType.MESH
BF16 = jnp.bfloat16
F32 = jnp.float32
BLOCKS = 4
HIDDEN = -1e30


def tables(tokens, rope, gain):
    half = rope // 2
    freq = np.exp(np.arange(half) * (-2.0 * math.log(10000.0) / rope))
    q_angle = np.arange(tokens)[:, None] * freq[None, :]
    q_cos = np.tile(np.cos(q_angle), (1, 4)).astype(np.float32)
    q_sin = np.tile(np.sin(q_angle), (1, 4)).astype(np.float32)
    k_place = np.arange(BLOCKS * tokens) - (BLOCKS - 1) * tokens
    k_angle = freq[:, None] * k_place[None, :]
    k_cos = (np.cos(k_angle) * gain).astype(np.float32)
    k_sin = (np.sin(k_angle) * gain).astype(np.float32)
    return q_cos, q_sin, k_cos, k_sin


def nt(a, b):
    return lax.dot_general(a, b, (((1,), (1,)), ((), ())), preferred_element_type=F32)


def nn(a, b):
    return jnp.dot(a, b, preferred_element_type=F32)


def kernel(
    n_ctx, n_head, gain,
    latent, prior, k_rope, seg, q_nope, q_rope, w_uk, w_uv, q_cos, q_sin, k_cos, k_sin,
    seen, own_out, own_top, qn, qx, kt, kx, vals, earlier_two, uk, uv, amax_out,
    lat, tops, z_tops, prior_v, seg_v, qr, qc, qs, kc, ks, clipped, kt3, vals3,
    own_recv, own_send, pair_recv, pair_send, side_recv, side_send, far_recv, far_send,
    sib_send, sib_recv, tops_recv, tops_send, z_recv, z_send, hello, load,
):
    ctx = lax.axis_index("ctx")
    me = lax.axis_index("head")
    core = lax.rem(ctx, 2)
    sibling = ctx + 1 - 2 * core
    n_z = n_ctx // 4
    z = ctx // 4
    heads, hd, width = uk.shape
    tokens = qn.shape[0]
    rope = k_rope.shape[0]
    rows = latent.shape[0]
    half = rope // 2
    mine = pl.ds(pl.multiple_of(me * rows, rows), rows)
    block = pl.ds(0, tokens)
    key_rows = pl.ds(tokens, half + 16)

    kind = lax.rem(ctx, 4)
    has1 = ctx >= 2
    has2 = (core == 1) | (ctx >= 2)
    has0 = ctx >= 3
    next2 = ctx + 2 < n_ctx
    next3 = (core == 1) & (ctx + 3 < n_ctx)

    beside = me + 1 - 2 * lax.rem(me, 2)
    up = lax.rem(me + 2, n_head)
    down = lax.rem(me + n_head - 2, n_head)

    def remote(src, dst, send, recv, c, h):
        return pltpu.make_async_remote_copy(
            src_ref=src, dst_ref=dst, send_sem=send, recv_sem=recv, device_id=(c, h), device_id_type=MESH
        )

    loads = [
        (latent, lat.at[3, mine]),
        (k_rope.at[pl.ds(0, half)], lat.at[3, pl.ds(tokens, half), pl.ds(0, tokens)]),
        (k_rope.at[pl.ds(half, half)], lat.at[3, pl.ds(tokens, half), pl.ds(tokens, tokens)]),
        (seg, seg_v), (prior, prior_v),
        (q_rope, qr), (q_cos, qc), (q_sin, qs), (k_cos, kc), (k_sin, ks), (w_uk, uk), (w_uv, uv), (q_nope, qn),
    ]
    loading = [pltpu.make_async_copy(src, dst, load.at[i]) for i, (src, dst) in enumerate(loads)]
    for copy in loading[:10]:
        copy.start()

    barrier = pltpu.get_barrier_semaphore()

    def greet(c, h):
        pl.semaphore_signal(barrier, inc=1, device_id=(c, h), device_id_type=MESH)

    @pl.when(has1)
    def _():
        greet(ctx - 2, me)
        greet(ctx - 2, beside)

    @pl.when((core == 0) & has0)
    def _():
        greet(ctx - 3, me)

    for k in range(1, n_head):
        greet(ctx, lax.rem(me + k, n_head))
    for d in (1, 2, 3):
        greet(4 * z + lax.rem(kind + d, 4), me)
    for k in range(1, n_z):
        pl.when(z + k < n_z)(functools.partial(greet, ctx + 4 * k, me))

    for slot, there in ((0, has0), (1, has1), (2, has2)):
        @pl.when(jnp.logical_not(there))
        def _(slot=slot):
            lat[slot, block, :] = jnp.zeros((tokens, width), BF16)
            lat[slot, key_rows, :] = jnp.full((half + 16, width), -1.0, BF16)

    for copy in loading[:4]:
        copy.wait()
    lat[3, pl.ds(tokens + half, 16), :] = jnp.broadcast_to(
        jnp.concatenate([seg_v[...], seg_v[...]], axis=1).astype(F32), (16, width)
    ).astype(BF16)
    listeners = 2 * next2.astype(jnp.int32) + next3.astype(jnp.int32)
    pl.semaphore_wait(barrier, n_head - 1 + 3 + z + listeners)

    def share(k):
        return remote(
            lat.at[3, mine], lat.at[3, mine], own_send, own_recv, ctx, lax.rem(me + k, n_head)
        )

    def chunk(slot, i, c, h):
        return remote(lat.at[3, mine], lat.at[slot, mine], pair_send.at[slot, i], pair_recv.at[slot, i], c, h)

    def keys_to(slot, c):
        return remote(lat.at[3, key_rows], lat.at[slot, key_rows], pair_send.at[slot, 2], pair_recv.at[slot, 2], c, me)

    ahead2 = [chunk(1, 0, ctx + 2, me), chunk(1, 1, ctx + 2, beside), keys_to(1, ctx + 2)]
    ahead3 = remote(lat.at[3], lat.at[0], sib_send.at[2], sib_recv.at[0], ctx + 3, me)

    @pl.when(next2)
    def _():
        for copy in ahead2:
            copy.start()

    for k in range(1, n_head):
        share(k).start()

    for copy in loading[10:]:
        copy.start()

    for k in range(1, n_z):
        @pl.when(z - k >= 0)
        def _(k=k):
            pl.semaphore_signal(hello, inc=1, device_id=(ctx - 4 * k, me), device_id_type=MESH)

    for copy in loading[4:10]:
        copy.wait()
    lane = lax.broadcasted_iota(jnp.int32, (tokens, 128), 1)
    docs = lax.broadcasted_iota(jnp.int32, (64, tokens), 0)
    docs = jnp.concatenate([docs, docs], axis=0)
    mark = (docs == jnp.broadcast_to(seg_v[...], (128, tokens))).astype(F32).T
    i = lax.broadcasted_iota(jnp.int32, (128, 128), 0)
    j = lax.broadcasted_iota(jnp.int32, (128, 128), 1)
    low = (j & 63) < 32
    swap = jnp.where(low & (i == j + 32), -1.0, jnp.where(jnp.logical_not(low) & (i == j - 32), 1.0, 0.0)).astype(BF16)
    cosine, sine = qc[...], qs[...]

    def turn(p, carry):
        raw = qr[:, pl.ds(pl.multiple_of(p * 128, 128), 128)]
        turned = raw.astype(F32) * cosine + nn(raw, swap) * sine
        qx[2 * p] = jnp.where(lane < 64, turned, mark).astype(BF16)
        qx[2 * p + 1] = jnp.where(lane < 64, mark, turned).astype(BF16)
        return carry

    lax.fori_loop(0, heads // 2, turn, 0, unroll=True)

    def pair_at(h):
        return pl.ds(pl.multiple_of(h // 2 * 2 * rows, 2 * rows), 2 * rows)

    def one_at(h, x):
        return pl.ds(pl.multiple_of((h // 2 * 2 + x) * rows, rows), rows)

    def side(slots, i, to):
        at = lat.at[slots, pair_at(me)]
        return remote(at, at, side_send.at[i], side_recv.at[i], ctx, to)

    def far(slots, i, h, to):
        at = lat.at[slots, one_at(h, i)]
        return remote(at, at, far_send.at[i], far_recv.at[i], ctx, to)

    def sides(slots):
        side(slots, 0, up).start()
        side(slots, 1, down).start()

    def fars(slots):
        side(slots, 0, up).wait_recv()
        far(slots, 0, down, up).start()
        side(slots, 1, down).wait_recv()
        far(slots, 1, up, down).start()

    def complete(slots):
        far(slots, 0, down, up).wait_recv()
        far(slots, 1, up, down).wait_recv()

    def sent(slots):
        for i in range(2):
            side(slots, i, up).wait_send()
            far(slots, i, up, up).wait_send()

    late = pl.ds(1, 1)

    def earlier(act):
        pl.when(has1)(functools.partial(act, late))

    @pl.when(has1)
    def _():
        for copy in ahead2:
            copy.wait_recv()

    earlier(sides)

    others = lat.at[3, pl.ds(0, (n_head - 1) * rows)]
    remote(others, others, own_send, own_recv, ctx, me).wait_recv()
    pass_own = remote(lat.at[3], lat.at[2], sib_send.at[0], sib_recv.at[2], sibling, me)
    pl.when(core == 0)(pass_own.start)
    pl.when(next3)(ahead3.start)
    tops[kind] = jnp.max(jnp.abs(lat[3, block, :].astype(F32)), axis=0, keepdims=True)

    def spread_top(d):
        return remote(tops.at[kind], tops.at[kind], tops_send, tops_recv, 4 * z + lax.rem(kind + d, 4), me)

    for d in (1, 2, 3):
        spread_top(d).start()

    earlier(fars)

    limit = prior_v[...].astype(BF16)
    for copy in loading[10:]:
        copy.wait()

    def project(slot):
        kt_to, vals_to = (kt3, vals3) if slot == 3 else (kt, vals)
        clipped[...] = jnp.clip(lat[slot, block, :], -limit, limit)

        def some(g, carry):
            c = clipped[...]
            ups = (nt(uk[pl.ds(4 * g, 4)].reshape(4 * hd, width), c) * gain).astype(BF16).reshape(4, hd, tokens)
            kt_to[pl.ds(4 * g, 4)] = ups
            for p in range(2):
                h = 4 * g + 2 * p
                both = nn(c, jnp.concatenate([uv[h], uv[h + 1]], axis=1)).astype(BF16)
                for e in range(2):
                    vals_to[h + e] = both[:, e * hd:(e + 1) * hd]
            return carry

        lax.fori_loop(0, heads // 4, some, 0, unroll=True)

    def turn_keys(slot):
        at = pl.ds(slot * tokens, tokens)
        a = lat[slot, pl.ds(tokens, half), 0:tokens].astype(F32)
        b = lat[slot, pl.ds(tokens, half), tokens:2 * tokens].astype(F32)
        cosine, sine = kc[:, at], ks[:, at]
        turned = jnp.concatenate([a * cosine - b * sine, b * cosine + a * sine], axis=0).astype(BF16)
        doc = jnp.broadcast_to(lat[slot, pl.ds(tokens + half, 16), 0:tokens].astype(F32)[0:1, :], (64, tokens))
        number = lax.broadcasted_iota(jnp.int32, (64, tokens), 0).astype(F32)
        other = jnp.where(doc == number, 0.0, HIDDEN).astype(BF16)
        kx[0, 0:64, at] = turned
        kx[0, 64:128, at] = other
        kx[1, 0:64, at] = other
        kx[1, 64:128, at] = turned

    project(3)

    three = tops.at[pl.ds(0, 3)]
    remote(three, three, tops_send, tops_recv, ctx, me).wait_recv()
    z_tops[z] = jnp.max(tops[...], axis=0)
    pl.when(z < n_z - 1)(lambda: pl.semaphore_wait(hello, n_z - 1 - z))

    def spread_z(k):
        return remote(z_tops.at[z], z_tops.at[z], z_send, z_recv, 4 * lax.rem(z + k, n_z) + kind, me)

    for k in range(1, n_z):
        spread_z(k).start()

    turn_keys(3)

    earlier(complete)
    on = [
        ((core == 0) & has1, remote(lat.at[1], lat.at[0], sib_send.at[1], sib_recv.at[0], sibling, me)),
        ((core == 1) & has1, remote(lat.at[1], lat.at[2], sib_send.at[1], sib_recv.at[2], sibling, me)),
    ]
    for there, copy in on:
        pl.when(there)(copy.start)

    q_at = lax.broadcasted_iota(jnp.int32, (tokens, tokens), 0)
    k_at = lax.broadcasted_iota(jnp.int32, (tokens, tokens), 1)

    def attend_own(first):
        for h in range(first, first + heads // 2):
            q = jnp.concatenate([qn[:, h * hd:(h + 1) * hd], qx[h]], axis=1)
            k = jnp.concatenate([kt3[h], kx[h % 2, :, 3 * tokens:]], axis=0)
            s = jnp.where(k_at <= q_at, nn(q, k), HIDDEN)
            top = jnp.max(s, axis=1, keepdims=True)
            w = jnp.exp2(s - top).astype(BF16)
            own_out[h] = nn(w, jnp.concatenate([vals3[h], jnp.ones((tokens, hd), BF16)], axis=1))
            own_top[h] = jnp.broadcast_to(top, (tokens, hd))

    attend_own(0)
    attend_own(heads // 2)

    earlier_two[1] = jnp.clip(lat[1, block, :], -limit, limit)
    turn_keys(1)

    pl.when(has2)(pass_own.wait_recv)
    project(2)
    turn_keys(2)

    pl.when(has0)(ahead3.wait_recv)
    earlier_two[0] = jnp.clip(lat[0, block, :], -limit, limit)
    turn_keys(0)

    doc_at = pl.ds(tokens + half, 16)
    doc = lat[3, doc_at, 0:tokens].astype(F32)[0:1, 0:1]
    count = jnp.zeros((1, 1), F32)
    for slot in range(3):
        count += (lat[slot, doc_at, 0:tokens].astype(F32)[0:1, tokens - 1:] == doc).astype(F32)
    wide = (lat[3, doc_at, 0:tokens].astype(F32)[0:1, tokens // 2:tokens // 2 + 1] == doc).astype(F32)
    seen[...] = jnp.broadcast_to(count + 4.0 * wide, seen.shape)

    rest = z_tops.at[pl.ds(0, n_z - 1)]
    remote(rest, rest, z_send, z_recv, ctx, me).wait_recv()
    amax_out[...] = jnp.max(z_tops[...], axis=0)

    remote(others, others, own_send, own_recv, ctx, me).wait_send()
    remote(three, three, tops_send, tops_recv, ctx, me).wait_send()
    remote(rest, rest, z_send, z_recv, ctx, me).wait_send()
    earlier(sent)

    @pl.when(next2)
    def _():
        for copy in ahead2:
            copy.wait_send()

    pl.when(next3)(ahead3.wait_send)
    pl.when(core == 0)(pass_own.wait_send)
    pl.when(has1)(on[0][1].wait_send)


def attend(
    gain, seen, own_out, own_top, qn, qx, kt, kx, vals, earlier_two, uk, uv, amax,
    out, amax_out, kt_two, vals_two, outs, store, amax_store,
):
    heads, hd, width = uk.shape
    tokens = qn.shape[0]
    write_amax = pltpu.make_async_copy(amax, amax_out, amax_store)
    write_amax.start()
    code = jnp.max(seen[...]).astype(jnp.int32)
    count = code & 3
    middle = tokens // 2
    together = min(heads, 8)

    def write(p):
        some = pl.ds(pl.multiple_of(p * 4 * hd, 4 * hd), 4 * hd)
        return pltpu.make_async_copy(outs.at[:, some], out.at[:, some], store.at[p])

    for slot in range(2):
        @pl.when(count >= 3 - slot)
        def _(slot=slot):
            def some(g, carry):
                c = earlier_two[slot]
                ups = nt(uk[pl.ds(4 * g, 4)].reshape(4 * hd, width), c) * gain
                kt_two[slot, pl.ds(4 * g, 4)] = ups.astype(BF16).reshape(4, hd, tokens)
                for p in range(2):
                    h = 4 * g + 2 * p
                    both = nn(c, jnp.concatenate([uv[h], uv[h + 1]], axis=1)).astype(BF16)
                    vals_two[slot, h] = both[:, :hd]
                    vals_two[slot, h + 1] = both[:, hd:]
                return carry

            lax.fori_loop(0, heads // 4, some, 0, unroll=True)

    def with_blocks(blocks, wide):
        seeing = 0 if not blocks else tokens if wide else middle
        skip = middle if wide and blocks == 3 else 0

        def group(g, carry):
            for i in range(together):
                h = together * g + i
                e = i % 2
                cols = pl.ds(pl.multiple_of(h * hd, hd), hd)
                if blocks:
                    q = jnp.concatenate([qn[0:seeing, cols], qx[h, 0:seeing, :]], axis=1)
                    k = [kt_two[x, h] for x in range(3 - blocks, 2)] + [kt[h]]
                    v = [vals_two[x, h] for x in range(3 - blocks, 2)] + [vals[h]]
                    k[0], v[0] = k[0][:, skip:], v[0][skip:]
                    k = jnp.concatenate(k, axis=1)
                    v = jnp.concatenate(v, axis=0)
                    k = jnp.concatenate([k, kx[e, :, (3 - blocks) * tokens + skip:3 * tokens]], axis=0)
                    s = nn(q, k)
                    own = own_top[h, 0:seeing, :]
                    top = jnp.maximum(jnp.broadcast_to(jnp.max(s, axis=1, keepdims=True), own.shape), own)
                    w = jnp.exp2(s - jnp.concatenate([top] * (s.shape[1] // hd), axis=1)).astype(BF16)
                    scale = jnp.exp2(own - top)
                    o = own_out[h, 0:seeing, :] * jnp.concatenate([scale, scale], axis=1) + nn(
                        w, jnp.concatenate([v, jnp.ones(v.shape, BF16)], axis=1)
                    )
                    outs[0:seeing, cols] = (o[:, :hd] / o[:, hd:]).astype(BF16)
                if seeing < tokens:
                    o = own_out[h, seeing:, :]
                    outs[seeing:, cols] = (o[:, :hd] / o[:, hd:]).astype(BF16)
                if i % 4 == 3:
                    write(together // 4 * g + i // 4).start()
            return carry

        lax.fori_loop(0, heads // together, group, 0)

    pl.when(count == 0)(functools.partial(with_blocks, 0, False))
    for blocks in range(1, 4):
        for wide in (False, True):
            pl.when(code == blocks + 4 * wide)(functools.partial(with_blocks, blocks, wide))

    def written(p, carry):
        write(p).wait()
        return carry

    lax.fori_loop(0, heads // 4, written, 0)
    write_amax.wait()


def shards(n_ctx, n_head, q_nope, q_rope, latent, amax_prior, k_rope, w_uk, w_uv, seg_ids):
    tokens, columns = q_nope.shape
    heads, hd, width = w_uk.shape
    rope = k_rope.shape[0]
    rows = latent.shape[0]
    gain = math.log2(math.e) * (hd + rope) ** -0.5
    q_cos, q_sin, k_cos, k_sin = tables(tokens, rope, gain)
    n_z = n_ctx // 4
    keys = BLOCKS * tokens
    dma = pltpu.SemaphoreType.DMA
    anywhere = pl.BlockSpec(memory_space=pl.ANY)
    in_vmem = pl.BlockSpec(memory_space=pltpu.VMEM)
    mib = 1024 * 1024
    operands = (
        latent, amax_prior.reshape(1, width), k_rope, seg_ids.reshape(1, tokens), q_nope, q_rope, w_uk, w_uv,
        jnp.asarray(q_cos), jnp.asarray(q_sin), jnp.asarray(k_cos), jnp.asarray(k_sin),
    )
    results = pl.pallas_call(
        functools.partial(kernel, n_ctx, n_head, gain),
        out_shape=(
            pltpu.VMEM((8, 128), F32),
            pltpu.VMEM((heads, tokens, 2 * hd), F32),
            pltpu.VMEM((heads, tokens, hd), F32),
            pltpu.VMEM((tokens, columns), BF16),
            pltpu.VMEM((heads, tokens, 128), BF16),
            pltpu.VMEM((heads, hd, tokens), BF16),
            pltpu.VMEM((2, 128, keys), BF16),
            pltpu.VMEM((heads, tokens, hd), BF16),
            pltpu.VMEM((2, tokens, width), BF16),
            pltpu.VMEM((heads, hd, width), BF16),
            pltpu.VMEM((heads, width, hd), BF16),
            pltpu.VMEM((1, width), F32),
        ),
        in_specs=[pl.BlockSpec(memory_space=pltpu.HBM)] * 12,
        out_specs=(in_vmem,) * 12,
        scratch_shapes=[
            pltpu.VMEM((BLOCKS, tokens + rope // 2 + 16, width), BF16),
            pltpu.VMEM((4, 1, width), F32),
            pltpu.VMEM((n_z, 1, width), F32),
            pltpu.VMEM((1, width), F32),
            pltpu.VMEM((1, tokens), jnp.int32),
            pltpu.VMEM((tokens, heads * rope), BF16),
            pltpu.VMEM(q_cos.shape, F32),
            pltpu.VMEM(q_sin.shape, F32),
            pltpu.VMEM(k_cos.shape, F32),
            pltpu.VMEM(k_sin.shape, F32),
            pltpu.VMEM((tokens, width), BF16),
            pltpu.VMEM((heads, hd, tokens), BF16),
            pltpu.VMEM((heads, tokens, hd), BF16),
            dma,
            dma,
            dma((2, 3)),
            dma((2, 3)),
            dma((2,)),
            dma((2,)),
            dma((2,)),
            dma((2,)),
            dma((3,)),
            dma((BLOCKS,)),
            dma,
            dma,
            dma,
            dma,
            pltpu.SemaphoreType.REGULAR,
            dma((13,)),
        ],
        compiler_params=pltpu.CompilerParams(collective_id=0, has_side_effects=True, vmem_limit_bytes=18 * mib),
        cost_estimate=pl.CostEstimate(flops=4_000_000_000, bytes_accessed=8_000_000, transcendentals=0),
    )(*(pltpu.with_memory_space_constraint(x, pltpu.HBM) for x in operands))
    attended, latent_amax = pl.pallas_call(
        functools.partial(attend, gain),
        out_shape=(jax.ShapeDtypeStruct((tokens, columns), BF16), jax.ShapeDtypeStruct((1, width), F32)),
        in_specs=[in_vmem] * 12,
        out_specs=(anywhere, anywhere),
        scratch_shapes=[
            pltpu.VMEM((2, heads, hd, tokens), BF16),
            pltpu.VMEM((2, heads, tokens, hd), BF16),
            pltpu.VMEM((tokens, columns), BF16),
            dma((heads // 4,)),
            dma,
        ],
        compiler_params=pltpu.CompilerParams(vmem_limit_bytes=18 * mib),
        cost_estimate=pl.CostEstimate(flops=10_000_000_000, bytes_accessed=8_000_000, transcendentals=4_194_304),
    )(*(pltpu.with_memory_space_constraint(x, pltpu.VMEM) for x in results))
    return attended, latent_amax.reshape(width)


def solution(mesh):
    placed = (
        P("ctx", "head"),
        P("ctx", "head"),
        P(("ctx", "head"), None),
        P(),
        P(None, "ctx"),
        P("head", None, None),
        P("head", None, None),
        P("ctx"),
    )
    return jax.shard_map(
        functools.partial(shards, mesh.shape["ctx"], mesh.shape["head"]),
        mesh=mesh, in_specs=placed, out_specs=(P("ctx", "head"), P()), check_vma=False,
    )
```

```python
import functools
import math

import jax
import jax.numpy as jnp
import numpy as np
from jax import lax
from jax.experimental import pallas as pl
from jax.experimental.pallas import tpu as pltpu
from jax.sharding import PartitionSpec as P

MESH = pl.DeviceIdType.MESH
BF16 = jnp.bfloat16
F32 = jnp.float32
BLOCKS = 4
HIDDEN = -1e30


def tables(tokens, rope, gain):
    half = rope // 2
    freq = np.exp(np.arange(half) * (-2.0 * math.log(10000.0) / rope))
    q_angle = np.arange(tokens)[:, None] * freq[None, :]
    q_cos = np.tile(np.cos(q_angle), (1, 4)).astype(np.float32)
    q_sin = np.tile(np.sin(q_angle), (1, 4)).astype(np.float32)
    k_place = np.arange(BLOCKS * tokens) - (BLOCKS - 1) * tokens
    k_angle = freq[:, None] * k_place[None, :]
    k_cos = (np.cos(k_angle) * gain).astype(np.float32)
    k_sin = (np.sin(k_angle) * gain).astype(np.float32)
    return q_cos, q_sin, k_cos, k_sin


def nt(a, b):
    return lax.dot_general(a, b, (((1,), (1,)), ((), ())), preferred_element_type=F32)


def nn(a, b):
    return jnp.dot(a, b, preferred_element_type=F32)


def kernel(
    n_ctx, n_head, gain,
    latent, prior, k_rope, seg, q_nope, q_rope, w_uk, w_uv, q_cos, q_sin, k_cos, k_sin,
    seen, own_out, own_top, qn, qx, kt, kx, vals, earlier_two, uk, uv, amax_out,
    lat, tops, z_tops, prior_v, seg_v, qr, qc, qs, kc, ks, clipped, kt3, vals3,
    own_recv, own_send, pair_recv, pair_send, side_recv, side_send, far_recv, far_send,
    sib_send, sib_recv, tops_recv, tops_send, z_recv, z_send, hello, load,
):
    ctx = lax.axis_index("ctx")
    me = lax.axis_index("head")
    core = lax.rem(ctx, 2)
    sibling = ctx + 1 - 2 * core
    n_z = n_ctx // 4
    z = ctx // 4
    heads, hd, width = uk.shape
    tokens = qn.shape[0]
    rope = k_rope.shape[0]
    rows = latent.shape[0]
    half = rope // 2
    mine = pl.ds(pl.multiple_of(me * rows, rows), rows)
    block = pl.ds(0, tokens)
    key_rows = pl.ds(tokens, half + 16)

    kind = lax.rem(ctx, 4)
    has1 = ctx >= 2
    has2 = (core == 1) | (ctx >= 2)
    has0 = ctx >= 3
    next2 = ctx + 2 < n_ctx
    next3 = (core == 1) & (ctx + 3 < n_ctx)

    beside = me + 1 - 2 * lax.rem(me, 2)
    up = lax.rem(me + 2, n_head)
    down = lax.rem(me + n_head - 2, n_head)

    def remote(src, dst, send, recv, c, h):
        return pltpu.make_async_remote_copy(
            src_ref=src, dst_ref=dst, send_sem=send, recv_sem=recv, device_id=(c, h), device_id_type=MESH
        )

    loads = [
        (latent, lat.at[3, mine]),
        (k_rope.at[pl.ds(0, half)], lat.at[3, pl.ds(tokens, half), pl.ds(0, tokens)]),
        (k_rope.at[pl.ds(half, half)], lat.at[3, pl.ds(tokens, half), pl.ds(tokens, tokens)]),
        (seg, seg_v), (prior, prior_v),
        (q_rope, qr), (q_cos, qc), (q_sin, qs), (k_cos, kc), (k_sin, ks), (w_uk, uk), (w_uv, uv), (q_nope, qn),
    ]
    loading = [pltpu.make_async_copy(src, dst, load.at[i]) for i, (src, dst) in enumerate(loads)]
    for copy in loading[:10]:
        copy.start()

    barrier = pltpu.get_barrier_semaphore()

    def greet(c, h):
        pl.semaphore_signal(barrier, inc=1, device_id=(c, h), device_id_type=MESH)

    @pl.when(has1)
    def _():
        greet(ctx - 2, me)
        greet(ctx - 2, beside)

    @pl.when((core == 0) & has0)
    def _():
        greet(ctx - 3, me)

    for k in range(1, n_head):
        greet(ctx, lax.rem(me + k, n_head))
    for d in (1, 2, 3):
        greet(4 * z + lax.rem(kind + d, 4), me)
    for k in range(1, n_z):
        pl.when(z + k < n_z)(functools.partial(greet, ctx + 4 * k, me))

    for slot, there in ((0, has0), (1, has1), (2, has2)):
        @pl.when(jnp.logical_not(there))
        def _(slot=slot):
            lat[slot, block, :] = jnp.zeros((tokens, width), BF16)
            lat[slot, key_rows, :] = jnp.full((half + 16, width), -1.0, BF16)

    for copy in loading[:4]:
        copy.wait()
    lat[3, pl.ds(tokens + half, 16), :] = jnp.broadcast_to(
        jnp.concatenate([seg_v[...], seg_v[...]], axis=1).astype(F32), (16, width)
    ).astype(BF16)
    listeners = 2 * next2.astype(jnp.int32) + next3.astype(jnp.int32)
    pl.semaphore_wait(barrier, n_head - 1 + 3 + z + listeners)

    def share(k):
        return remote(
            lat.at[3, mine], lat.at[3, mine], own_send, own_recv, ctx, lax.rem(me + k, n_head)
        )

    def chunk(slot, i, c, h):
        return remote(lat.at[3, mine], lat.at[slot, mine], pair_send.at[slot, i], pair_recv.at[slot, i], c, h)

    def keys_to(slot, c):
        return remote(lat.at[3, key_rows], lat.at[slot, key_rows], pair_send.at[slot, 2], pair_recv.at[slot, 2], c, me)

    ahead2 = [chunk(1, 0, ctx + 2, me), chunk(1, 1, ctx + 2, beside), keys_to(1, ctx + 2)]
    ahead3 = remote(lat.at[3], lat.at[0], sib_send.at[2], sib_recv.at[0], ctx + 3, me)

    for k in range(1, n_head):
        share(k).start()

    @pl.when(next2)
    def _():
        for copy in ahead2:
            copy.start()

    for copy in loading[10:]:
        copy.start()

    for k in range(1, n_z):
        @pl.when(z - k >= 0)
        def _(k=k):
            pl.semaphore_signal(hello, inc=1, device_id=(ctx - 4 * k, me), device_id_type=MESH)

    def pair_at(h):
        return pl.ds(pl.multiple_of(h // 2 * 2 * rows, 2 * rows), 2 * rows)

    def one_at(h, x):
        return pl.ds(pl.multiple_of((h // 2 * 2 + x) * rows, rows), rows)

    def side(slots, i, to):
        at = lat.at[slots, pair_at(me)]
        return remote(at, at, side_send.at[i], side_recv.at[i], ctx, to)

    def far(slots, i, h, to):
        at = lat.at[slots, one_at(h, i)]
        return remote(at, at, far_send.at[i], far_recv.at[i], ctx, to)

    def sides(slots):
        side(slots, 0, up).start()
        side(slots, 1, down).start()

    def fars(slots):
        side(slots, 0, up).wait_recv()
        far(slots, 0, down, up).start()
        side(slots, 1, down).wait_recv()
        far(slots, 1, up, down).start()

    def complete(slots):
        far(slots, 0, down, up).wait_recv()
        far(slots, 1, up, down).wait_recv()

    def sent(slots):
        for i in range(2):
            side(slots, i, up).wait_send()
            far(slots, i, up, up).wait_send()

    late = pl.ds(1, 1)

    def earlier(act):
        pl.when(has1)(functools.partial(act, late))

    @pl.when(has1)
    def _():
        for copy in ahead2:
            copy.wait_recv()

    earlier(sides)

    others = lat.at[3, pl.ds(0, (n_head - 1) * rows)]
    remote(others, others, own_send, own_recv, ctx, me).wait_recv()
    pass_own = remote(lat.at[3], lat.at[2], sib_send.at[0], sib_recv.at[2], sibling, me)
    pl.when(core == 0)(pass_own.start)
    pl.when(next3)(ahead3.start)
    tops[kind] = jnp.max(jnp.abs(lat[3, block, :].astype(F32)), axis=0, keepdims=True)

    def spread_top(d):
        return remote(tops.at[kind], tops.at[kind], tops_send, tops_recv, 4 * z + lax.rem(kind + d, 4), me)

    for d in (1, 2, 3):
        spread_top(d).start()

    for copy in loading[4:10]:
        copy.wait()
    lane = lax.broadcasted_iota(jnp.int32, (tokens, 128), 1)
    docs = lax.broadcasted_iota(jnp.int32, (64, tokens), 0)
    docs = jnp.concatenate([docs, docs], axis=0)
    mark = (docs == jnp.broadcast_to(seg_v[...], (128, tokens))).astype(F32).T
    i = lax.broadcasted_iota(jnp.int32, (128, 128), 0)
    j = lax.broadcasted_iota(jnp.int32, (128, 128), 1)
    low = (j & 63) < 32
    swap = jnp.where(low & (i == j + 32), -1.0, jnp.where(jnp.logical_not(low) & (i == j - 32), 1.0, 0.0)).astype(BF16)
    cosine, sine = qc[...], qs[...]

    def turn(p, carry):
        raw = qr[:, pl.ds(pl.multiple_of(p * 128, 128), 128)]
        turned = raw.astype(F32) * cosine + nn(raw, swap) * sine
        qx[2 * p] = jnp.where(lane < 64, turned, mark).astype(BF16)
        qx[2 * p + 1] = jnp.where(lane < 64, mark, turned).astype(BF16)
        return carry

    lax.fori_loop(0, heads // 2, turn, 0, unroll=True)

    earlier(fars)

    three = tops.at[pl.ds(0, 3)]
    remote(three, three, tops_send, tops_recv, ctx, me).wait_recv()
    z_tops[z] = jnp.max(tops[...], axis=0)

    def spread_z(k):
        return remote(z_tops.at[z], z_tops.at[z], z_send.at[k + n_z], z_recv, ctx + 4 * k, me)

    for k in range(1, n_z):
        pl.when(z - k >= 0)(spread_z(-k).start)

    limit = prior_v[...].astype(BF16)
    for copy in loading[10:]:
        copy.wait()

    def project(slot):
        kt_to, vals_to = (kt3, vals3) if slot == 3 else (kt, vals)
        clipped[...] = jnp.clip(lat[slot, block, :], -limit, limit)

        def some(g, carry):
            c = clipped[...]
            ups = (nt(uk[pl.ds(4 * g, 4)].reshape(4 * hd, width), c) * gain).astype(BF16).reshape(4, hd, tokens)
            kt_to[pl.ds(4 * g, 4)] = ups
            for p in range(2):
                h = 4 * g + 2 * p
                both = nn(c, jnp.concatenate([uv[h], uv[h + 1]], axis=1)).astype(BF16)
                for e in range(2):
                    vals_to[h + e] = both[:, e * hd:(e + 1) * hd]
            return carry

        lax.fori_loop(0, heads // 4, some, 0, unroll=True)

    def turn_keys(slot):
        at = pl.ds(slot * tokens, tokens)
        a = lat[slot, pl.ds(tokens, half), 0:tokens].astype(F32)
        b = lat[slot, pl.ds(tokens, half), tokens:2 * tokens].astype(F32)
        cosine, sine = kc[:, at], ks[:, at]
        turned = jnp.concatenate([a * cosine - b * sine, b * cosine + a * sine], axis=0).astype(BF16)
        doc = jnp.broadcast_to(lat[slot, pl.ds(tokens + half, 16), 0:tokens].astype(F32)[0:1, :], (64, tokens))
        number = lax.broadcasted_iota(jnp.int32, (64, tokens), 0).astype(F32)
        other = jnp.where(doc == number, 0.0, HIDDEN).astype(BF16)
        kx[0, 0:64, at] = turned
        kx[0, 64:128, at] = other
        kx[1, 0:64, at] = other
        kx[1, 64:128, at] = turned

    project(3)

    turn_keys(3)

    earlier(complete)
    on = [
        ((core == 0) & has1, remote(lat.at[1], lat.at[0], sib_send.at[1], sib_recv.at[0], sibling, me)),
        ((core == 1) & has1, remote(lat.at[1], lat.at[2], sib_send.at[1], sib_recv.at[2], sibling, me)),
    ]
    for there, copy in on:
        pl.when(there)(copy.start)

    q_at = lax.broadcasted_iota(jnp.int32, (tokens, tokens), 0)
    k_at = lax.broadcasted_iota(jnp.int32, (tokens, tokens), 1)

    def attend_own(first):
        for h in range(first, first + heads // 2):
            q = jnp.concatenate([qn[:, h * hd:(h + 1) * hd], qx[h]], axis=1)
            k = jnp.concatenate([kt3[h], kx[h % 2, :, 3 * tokens:]], axis=0)
            s = jnp.where(k_at <= q_at, nn(q, k), HIDDEN)
            top = jnp.max(s, axis=1, keepdims=True)
            w = jnp.exp2(s - top).astype(BF16)
            own_out[h] = nn(w, jnp.concatenate([vals3[h], jnp.ones((tokens, hd), BF16)], axis=1))
            own_top[h] = jnp.broadcast_to(top, (tokens, hd))

    attend_own(0)

    @pl.when(z < n_z - 1)
    def _():
        pl.semaphore_wait(hello, n_z - 1 - z)
        for k in range(1, n_z):
            pl.when(z + k < n_z)(spread_z(k).start)

    attend_own(heads // 2)

    earlier_two[1] = jnp.clip(lat[1, block, :], -limit, limit)
    turn_keys(1)

    pl.when(has2)(pass_own.wait_recv)
    project(2)
    turn_keys(2)

    pl.when(has0)(ahead3.wait_recv)
    earlier_two[0] = jnp.clip(lat[0, block, :], -limit, limit)
    turn_keys(0)

    doc_at = pl.ds(tokens + half, 16)
    doc = lat[3, doc_at, 0:tokens].astype(F32)[0:1, 0:1]
    count = jnp.zeros((1, 1), F32)
    for slot in range(3):
        count += (lat[slot, doc_at, 0:tokens].astype(F32)[0:1, tokens - 1:] == doc).astype(F32)
    wide = (lat[3, doc_at, 0:tokens].astype(F32)[0:1, tokens // 2:tokens // 2 + 1] == doc).astype(F32)
    seen[...] = jnp.broadcast_to(count + 4.0 * wide, seen.shape)

    rest = z_tops.at[pl.ds(0, n_z - 1)]
    remote(rest, rest, z_send.at[0], z_recv, ctx, me).wait_recv()
    amax_out[...] = jnp.max(z_tops[...], axis=0)

    remote(others, others, own_send, own_recv, ctx, me).wait_send()
    remote(three, three, tops_send, tops_recv, ctx, me).wait_send()
    for k in range(1, n_z):
        pl.when(z - k >= 0)(spread_z(-k).wait_send)
        pl.when(z + k < n_z)(spread_z(k).wait_send)
    earlier(sent)

    @pl.when(next2)
    def _():
        for copy in ahead2:
            copy.wait_send()

    pl.when(next3)(ahead3.wait_send)
    pl.when(core == 0)(pass_own.wait_send)
    pl.when(has1)(on[0][1].wait_send)


def attend(
    gain, seen, own_out, own_top, qn, qx, kt, kx, vals, earlier_two, uk, uv, amax,
    out, amax_out, kt_two, vals_two, outs, store, amax_store,
):
    heads, hd, width = uk.shape
    tokens = qn.shape[0]
    write_amax = pltpu.make_async_copy(amax, amax_out, amax_store)
    write_amax.start()
    code = jnp.max(seen[...]).astype(jnp.int32)
    count = code & 3
    middle = tokens // 2
    together = min(heads, 8)

    def write(p):
        some = pl.ds(pl.multiple_of(p * 4 * hd, 4 * hd), 4 * hd)
        return pltpu.make_async_copy(outs.at[:, some], out.at[:, some], store.at[p])

    for slot in range(2):
        @pl.when(count >= 3 - slot)
        def _(slot=slot):
            def some(g, carry):
                c = earlier_two[slot]
                ups = nt(uk[pl.ds(4 * g, 4)].reshape(4 * hd, width), c) * gain
                kt_two[slot, pl.ds(4 * g, 4)] = ups.astype(BF16).reshape(4, hd, tokens)
                for p in range(2):
                    h = 4 * g + 2 * p
                    both = nn(c, jnp.concatenate([uv[h], uv[h + 1]], axis=1)).astype(BF16)
                    vals_two[slot, h] = both[:, :hd]
                    vals_two[slot, h + 1] = both[:, hd:]
                return carry

            lax.fori_loop(0, heads // 4, some, 0, unroll=True)

    def with_blocks(blocks, wide):
        seeing = 0 if not blocks else tokens if wide else middle
        skip = middle if wide and blocks == 3 else 0

        def group(g, carry):
            for i in range(together):
                h = together * g + i
                e = i % 2
                cols = pl.ds(pl.multiple_of(h * hd, hd), hd)
                if blocks:
                    q = jnp.concatenate([qn[0:seeing, cols], qx[h, 0:seeing, :]], axis=1)
                    k = [kt_two[x, h] for x in range(3 - blocks, 2)] + [kt[h]]
                    v = [vals_two[x, h] for x in range(3 - blocks, 2)] + [vals[h]]
                    k[0], v[0] = k[0][:, skip:], v[0][skip:]
                    k = jnp.concatenate(k, axis=1)
                    v = jnp.concatenate(v, axis=0)
                    k = jnp.concatenate([k, kx[e, :, (3 - blocks) * tokens + skip:3 * tokens]], axis=0)
                    s = nn(q, k)
                    own = own_top[h, 0:seeing, :]
                    top = jnp.maximum(jnp.broadcast_to(jnp.max(s, axis=1, keepdims=True), own.shape), own)
                    w = jnp.exp2(s - jnp.concatenate([top] * (s.shape[1] // hd), axis=1)).astype(BF16)
                    scale = jnp.exp2(own - top)
                    o = own_out[h, 0:seeing, :] * jnp.concatenate([scale, scale], axis=1) + nn(
                        w, jnp.concatenate([v, jnp.ones(v.shape, BF16)], axis=1)
                    )
                    outs[0:seeing, cols] = (o[:, :hd] / o[:, hd:]).astype(BF16)
                if seeing < tokens:
                    o = own_out[h, seeing:, :]
                    outs[seeing:, cols] = (o[:, :hd] / o[:, hd:]).astype(BF16)
                if i % 4 == 3:
                    write(together // 4 * g + i // 4).start()
            return carry

        lax.fori_loop(0, heads // together, group, 0)

    pl.when(count == 0)(functools.partial(with_blocks, 0, False))
    for blocks in range(1, 4):
        for wide in (False, True):
            pl.when(code == blocks + 4 * wide)(functools.partial(with_blocks, blocks, wide))

    def written(p, carry):
        write(p).wait()
        return carry

    lax.fori_loop(0, heads // 4, written, 0)
    write_amax.wait()


def shards(n_ctx, n_head, q_nope, q_rope, latent, amax_prior, k_rope, w_uk, w_uv, seg_ids):
    tokens, columns = q_nope.shape
    heads, hd, width = w_uk.shape
    rope = k_rope.shape[0]
    rows = latent.shape[0]
    gain = math.log2(math.e) * (hd + rope) ** -0.5
    q_cos, q_sin, k_cos, k_sin = tables(tokens, rope, gain)
    n_z = n_ctx // 4
    keys = BLOCKS * tokens
    dma = pltpu.SemaphoreType.DMA
    anywhere = pl.BlockSpec(memory_space=pl.ANY)
    in_vmem = pl.BlockSpec(memory_space=pltpu.VMEM)
    mib = 1024 * 1024
    operands = (
        latent, amax_prior.reshape(1, width), k_rope, seg_ids.reshape(1, tokens), q_nope, q_rope, w_uk, w_uv,
        jnp.asarray(q_cos), jnp.asarray(q_sin), jnp.asarray(k_cos), jnp.asarray(k_sin),
    )
    results = pl.pallas_call(
        functools.partial(kernel, n_ctx, n_head, gain),
        out_shape=(
            pltpu.VMEM((8, 128), F32),
            pltpu.VMEM((heads, tokens, 2 * hd), F32),
            pltpu.VMEM((heads, tokens, hd), F32),
            pltpu.VMEM((tokens, columns), BF16),
            pltpu.VMEM((heads, tokens, 128), BF16),
            pltpu.VMEM((heads, hd, tokens), BF16),
            pltpu.VMEM((2, 128, keys), BF16),
            pltpu.VMEM((heads, tokens, hd), BF16),
            pltpu.VMEM((2, tokens, width), BF16),
            pltpu.VMEM((heads, hd, width), BF16),
            pltpu.VMEM((heads, width, hd), BF16),
            pltpu.VMEM((1, width), F32),
        ),
        in_specs=[pl.BlockSpec(memory_space=pltpu.HBM)] * 12,
        out_specs=(in_vmem,) * 12,
        scratch_shapes=[
            pltpu.VMEM((BLOCKS, tokens + rope // 2 + 16, width), BF16),
            pltpu.VMEM((4, 1, width), F32),
            pltpu.VMEM((n_z, 1, width), F32),
            pltpu.VMEM((1, width), F32),
            pltpu.VMEM((1, tokens), jnp.int32),
            pltpu.VMEM((tokens, heads * rope), BF16),
            pltpu.VMEM(q_cos.shape, F32),
            pltpu.VMEM(q_sin.shape, F32),
            pltpu.VMEM(k_cos.shape, F32),
            pltpu.VMEM(k_sin.shape, F32),
            pltpu.VMEM((tokens, width), BF16),
            pltpu.VMEM((heads, hd, tokens), BF16),
            pltpu.VMEM((heads, tokens, hd), BF16),
            dma,
            dma,
            dma((2, 3)),
            dma((2, 3)),
            dma((2,)),
            dma((2,)),
            dma((2,)),
            dma((2,)),
            dma((3,)),
            dma((BLOCKS,)),
            dma,
            dma,
            dma,
            dma((2 * n_z,)),
            pltpu.SemaphoreType.REGULAR,
            dma((13,)),
        ],
        compiler_params=pltpu.CompilerParams(collective_id=0, has_side_effects=True, vmem_limit_bytes=18 * mib),
        cost_estimate=pl.CostEstimate(flops=4_000_000_000, bytes_accessed=8_000_000, transcendentals=0),
    )(*(pltpu.with_memory_space_constraint(x, pltpu.HBM) for x in operands))
    attended, latent_amax = pl.pallas_call(
        functools.partial(attend, gain),
        out_shape=(jax.ShapeDtypeStruct((tokens, columns), BF16), jax.ShapeDtypeStruct((1, width), F32)),
        in_specs=[in_vmem] * 12,
        out_specs=(anywhere, anywhere),
        scratch_shapes=[
            pltpu.VMEM((2, heads, hd, tokens), BF16),
            pltpu.VMEM((2, heads, tokens, hd), BF16),
            pltpu.VMEM((tokens, columns), BF16),
            dma((heads // 4,)),
            dma,
        ],
        compiler_params=pltpu.CompilerParams(vmem_limit_bytes=18 * mib),
        cost_estimate=pl.CostEstimate(flops=10_000_000_000, bytes_accessed=8_000_000, transcendentals=4_194_304),
    )(*(pltpu.with_memory_space_constraint(x, pltpu.VMEM) for x in results))
    return attended, latent_amax.reshape(width)


def solution(mesh):
    placed = (
        P("ctx", "head"),
        P("ctx", "head"),
        P(("ctx", "head"), None),
        P(),
        P(None, "ctx"),
        P("head", None, None),
        P("head", None, None),
        P("ctx"),
    )
    return jax.shard_map(
        functools.partial(shards, mesh.shape["ctx"], mesh.shape["head"]),
        mesh=mesh, in_specs=placed, out_specs=(P("ctx", "head"), P()), check_vma=False,
    )
```

```python
import functools
import math

import jax
import jax.numpy as jnp
import numpy as np
from jax import lax
from jax.experimental import pallas as pl
from jax.experimental.pallas import tpu as pltpu
from jax.sharding import PartitionSpec as P

MESH = pl.DeviceIdType.MESH
BF16 = jnp.bfloat16
F32 = jnp.float32
BLOCKS = 4
HIDDEN = -1e30


def tables(tokens, rope, gain):
    half = rope // 2
    freq = np.exp(np.arange(half) * (-2.0 * math.log(10000.0) / rope))
    q_angle = np.arange(tokens)[:, None] * freq[None, :]
    q_cos = np.tile(np.cos(q_angle), (1, 4)).astype(np.float32)
    q_sin = np.tile(np.sin(q_angle), (1, 4)).astype(np.float32)
    k_place = np.arange(BLOCKS * tokens) - (BLOCKS - 1) * tokens
    k_angle = freq[:, None] * k_place[None, :]
    k_cos = (np.cos(k_angle) * gain).astype(np.float32)
    k_sin = (np.sin(k_angle) * gain).astype(np.float32)
    return q_cos, q_sin, k_cos, k_sin


def nt(a, b):
    return lax.dot_general(a, b, (((1,), (1,)), ((), ())), preferred_element_type=F32)


def nn(a, b):
    return jnp.dot(a, b, preferred_element_type=F32)


def kernel(
    n_ctx, n_head, gain,
    latent, prior, k_rope, seg, q_nope, q_rope, w_uk, w_uv, q_cos, q_sin, k_cos, k_sin,
    seen, own_out, own_top, qn, qx, kt, kx, vals, earlier_two, uk, uv, kt_two, vals_two, amax_out,
    lat, tops, z_tops, prior_v, seg_v, qr, qc, qs, kc, ks, clipped, kt3, vals3,
    own_recv, own_send, pair_recv, pair_send, side_recv, side_send, far_recv, far_send,
    sib_send, sib_recv, tops_recv, tops_send, z_recv, z_send, hello, load,
):
    ctx = lax.axis_index("ctx")
    me = lax.axis_index("head")
    core = lax.rem(ctx, 2)
    sibling = ctx + 1 - 2 * core
    n_z = n_ctx // 4
    z = ctx // 4
    heads, hd, width = uk.shape
    tokens = qn.shape[0]
    rope = k_rope.shape[0]
    rows = latent.shape[0]
    half = rope // 2
    mine = pl.ds(pl.multiple_of(me * rows, rows), rows)
    block = pl.ds(0, tokens)
    key_rows = pl.ds(tokens, half + 16)

    kind = lax.rem(ctx, 4)
    has1 = ctx >= 2
    has2 = (core == 1) | (ctx >= 2)
    has0 = ctx >= 3
    next2 = ctx + 2 < n_ctx
    next3 = (core == 1) & (ctx + 3 < n_ctx)

    beside = me + 1 - 2 * lax.rem(me, 2)
    up = lax.rem(me + 2, n_head)
    down = lax.rem(me + n_head - 2, n_head)

    def remote(src, dst, send, recv, c, h):
        return pltpu.make_async_remote_copy(
            src_ref=src, dst_ref=dst, send_sem=send, recv_sem=recv, device_id=(c, h), device_id_type=MESH
        )

    loads = [
        (latent, lat.at[3, mine]),
        (k_rope.at[pl.ds(0, half)], lat.at[3, pl.ds(tokens, half), pl.ds(0, tokens)]),
        (k_rope.at[pl.ds(half, half)], lat.at[3, pl.ds(tokens, half), pl.ds(tokens, tokens)]),
        (seg, seg_v), (prior, prior_v),
        (q_rope, qr), (q_cos, qc), (q_sin, qs), (k_cos, kc), (k_sin, ks), (w_uk, uk), (w_uv, uv), (q_nope, qn),
    ]
    loading = [pltpu.make_async_copy(src, dst, load.at[i]) for i, (src, dst) in enumerate(loads)]
    for copy in loading[:10]:
        copy.start()

    barrier = pltpu.get_barrier_semaphore()

    def greet(c, h):
        pl.semaphore_signal(barrier, inc=1, device_id=(c, h), device_id_type=MESH)

    @pl.when(has1)
    def _():
        greet(ctx - 2, me)
        greet(ctx - 2, beside)

    @pl.when((core == 0) & has0)
    def _():
        greet(ctx - 3, me)

    for k in range(1, n_head):
        greet(ctx, lax.rem(me + k, n_head))
    for d in (1, 2, 3):
        greet(4 * z + lax.rem(kind + d, 4), me)
    for k in range(1, n_z):
        pl.when(z + k < n_z)(functools.partial(greet, ctx + 4 * k, me))

    for slot, there in ((0, has0), (1, has1), (2, has2)):
        @pl.when(jnp.logical_not(there))
        def _(slot=slot):
            lat[slot, block, :] = jnp.zeros((tokens, width), BF16)
            lat[slot, key_rows, :] = jnp.full((half + 16, width), -1.0, BF16)

    for copy in loading[:4]:
        copy.wait()
    lat[3, pl.ds(tokens + half, 16), :] = jnp.broadcast_to(
        jnp.concatenate([seg_v[...], seg_v[...]], axis=1).astype(F32), (16, width)
    ).astype(BF16)
    listeners = 2 * next2.astype(jnp.int32) + next3.astype(jnp.int32)
    pl.semaphore_wait(barrier, n_head - 1 + 3 + z + listeners)

    def share(k):
        return remote(
            lat.at[3, mine], lat.at[3, mine], own_send, own_recv, ctx, lax.rem(me + k, n_head)
        )

    def chunk(slot, i, c, h):
        return remote(lat.at[3, mine], lat.at[slot, mine], pair_send.at[slot, i], pair_recv.at[slot, i], c, h)

    def keys_to(slot, c):
        return remote(lat.at[3, key_rows], lat.at[slot, key_rows], pair_send.at[slot, 2], pair_recv.at[slot, 2], c, me)

    ahead2 = [chunk(1, 0, ctx + 2, me), chunk(1, 1, ctx + 2, beside), keys_to(1, ctx + 2)]
    ahead3 = remote(lat.at[3], lat.at[0], sib_send.at[2], sib_recv.at[0], ctx + 3, me)

    for k in range(1, n_head):
        share(k).start()

    @pl.when(next2)
    def _():
        for copy in ahead2:
            copy.start()

    for copy in loading[10:]:
        copy.start()

    for k in range(1, n_z):
        @pl.when(z - k >= 0)
        def _(k=k):
            pl.semaphore_signal(hello, inc=1, device_id=(ctx - 4 * k, me), device_id_type=MESH)

    def pair_at(h):
        return pl.ds(pl.multiple_of(h // 2 * 2 * rows, 2 * rows), 2 * rows)

    def one_at(h, x):
        return pl.ds(pl.multiple_of((h // 2 * 2 + x) * rows, rows), rows)

    def side(slots, i, to):
        at = lat.at[slots, pair_at(me)]
        return remote(at, at, side_send.at[i], side_recv.at[i], ctx, to)

    def far(slots, i, h, to):
        at = lat.at[slots, one_at(h, i)]
        return remote(at, at, far_send.at[i], far_recv.at[i], ctx, to)

    def sides(slots):
        side(slots, 0, up).start()
        side(slots, 1, down).start()

    def fars(slots):
        side(slots, 0, up).wait_recv()
        far(slots, 0, down, up).start()
        side(slots, 1, down).wait_recv()
        far(slots, 1, up, down).start()

    def complete(slots):
        far(slots, 0, down, up).wait_recv()
        far(slots, 1, up, down).wait_recv()

    def sent(slots):
        for i in range(2):
            side(slots, i, up).wait_send()
            far(slots, i, up, up).wait_send()

    late = pl.ds(1, 1)

    def earlier(act):
        pl.when(has1)(functools.partial(act, late))

    @pl.when(has1)
    def _():
        for copy in ahead2:
            copy.wait_recv()

    earlier(sides)

    others = lat.at[3, pl.ds(0, (n_head - 1) * rows)]
    remote(others, others, own_send, own_recv, ctx, me).wait_recv()
    pass_own = remote(lat.at[3], lat.at[2], sib_send.at[0], sib_recv.at[2], sibling, me)
    pl.when(core == 0)(pass_own.start)
    pl.when(next3)(ahead3.start)
    tops[kind] = jnp.max(jnp.abs(lat[3, block, :].astype(F32)), axis=0, keepdims=True)

    def spread_top(d):
        return remote(tops.at[kind], tops.at[kind], tops_send, tops_recv, 4 * z + lax.rem(kind + d, 4), me)

    for d in (1, 2, 3):
        spread_top(d).start()

    for copy in loading[4:10]:
        copy.wait()
    lane = lax.broadcasted_iota(jnp.int32, (tokens, 128), 1)
    docs = lax.broadcasted_iota(jnp.int32, (64, tokens), 0)
    docs = jnp.concatenate([docs, docs], axis=0)
    mark = (docs == jnp.broadcast_to(seg_v[...], (128, tokens))).astype(F32).T
    i = lax.broadcasted_iota(jnp.int32, (128, 128), 0)
    j = lax.broadcasted_iota(jnp.int32, (128, 128), 1)
    low = (j & 63) < 32
    swap = jnp.where(low & (i == j + 32), -1.0, jnp.where(jnp.logical_not(low) & (i == j - 32), 1.0, 0.0)).astype(BF16)
    cosine, sine = qc[...], qs[...]

    def turn(p, carry):
        raw = qr[:, pl.ds(pl.multiple_of(p * 128, 128), 128)]
        turned = raw.astype(F32) * cosine + nn(raw, swap) * sine
        qx[2 * p] = jnp.where(lane < 64, turned, mark).astype(BF16)
        qx[2 * p + 1] = jnp.where(lane < 64, mark, turned).astype(BF16)
        return carry

    lax.fori_loop(0, heads // 2, turn, 0, unroll=True)

    earlier(fars)

    three = tops.at[pl.ds(0, 3)]
    remote(three, three, tops_send, tops_recv, ctx, me).wait_recv()
    z_tops[z] = jnp.max(tops[...], axis=0)

    def spread_z(k):
        return remote(z_tops.at[z], z_tops.at[z], z_send.at[k + n_z], z_recv, ctx + 4 * k, me)

    for k in range(1, n_z):
        pl.when(z - k >= 0)(spread_z(-k).start)

    limit = prior_v[...].astype(BF16)
    for copy in loading[10:]:
        copy.wait()

    def project(slot):
        kt_to, vals_to = (kt3, vals3) if slot == 3 else (kt, vals) if slot == 2 else (kt_two.at[slot], vals_two.at[slot])
        clipped[...] = jnp.clip(lat[slot, block, :], -limit, limit)

        def some(g, carry):
            c = clipped[...]
            ups = (nt(uk[pl.ds(4 * g, 4)].reshape(4 * hd, width), c) * gain).astype(BF16).reshape(4, hd, tokens)
            kt_to[pl.ds(4 * g, 4)] = ups
            for p in range(2):
                h = 4 * g + 2 * p
                both = nn(c, jnp.concatenate([uv[h], uv[h + 1]], axis=1)).astype(BF16)
                for e in range(2):
                    vals_to[h + e] = both[:, e * hd:(e + 1) * hd]
            return carry

        lax.fori_loop(0, heads // 4, some, 0, unroll=True)

    def turn_keys(slot):
        at = pl.ds(slot * tokens, tokens)
        a = lat[slot, pl.ds(tokens, half), 0:tokens].astype(F32)
        b = lat[slot, pl.ds(tokens, half), tokens:2 * tokens].astype(F32)
        cosine, sine = kc[:, at], ks[:, at]
        turned = jnp.concatenate([a * cosine - b * sine, b * cosine + a * sine], axis=0).astype(BF16)
        doc = jnp.broadcast_to(lat[slot, pl.ds(tokens + half, 16), 0:tokens].astype(F32)[0:1, :], (64, tokens))
        number = lax.broadcasted_iota(jnp.int32, (64, tokens), 0).astype(F32)
        other = jnp.where(doc == number, 0.0, HIDDEN).astype(BF16)
        kx[0, 0:64, at] = turned
        kx[0, 64:128, at] = other
        kx[1, 0:64, at] = other
        kx[1, 64:128, at] = turned

    project(3)

    turn_keys(3)

    earlier(complete)
    on = [
        ((core == 0) & has1, remote(lat.at[1], lat.at[0], sib_send.at[1], sib_recv.at[0], sibling, me)),
        ((core == 1) & has1, remote(lat.at[1], lat.at[2], sib_send.at[1], sib_recv.at[2], sibling, me)),
    ]
    for there, copy in on:
        pl.when(there)(copy.start)

    q_at = lax.broadcasted_iota(jnp.int32, (tokens, tokens), 0)
    k_at = lax.broadcasted_iota(jnp.int32, (tokens, tokens), 1)

    def attend_own(first):
        for h in range(first, first + heads // 2):
            q = jnp.concatenate([qn[:, h * hd:(h + 1) * hd], qx[h]], axis=1)
            k = jnp.concatenate([kt3[h], kx[h % 2, :, 3 * tokens:]], axis=0)
            s = jnp.where(k_at <= q_at, nn(q, k), HIDDEN)
            top = jnp.max(s, axis=1, keepdims=True)
            w = jnp.exp2(s - top).astype(BF16)
            own_out[h] = nn(w, jnp.concatenate([vals3[h], jnp.ones((tokens, hd), BF16)], axis=1))
            own_top[h] = jnp.broadcast_to(top, (tokens, hd))

    attend_own(0)

    @pl.when(z < n_z - 1)
    def _():
        pl.semaphore_wait(hello, n_z - 1 - z)
        for k in range(1, n_z):
            pl.when(z + k < n_z)(spread_z(k).start)

    attend_own(heads // 2)

    earlier_two[1] = jnp.clip(lat[1, block, :], -limit, limit)
    turn_keys(1)

    pl.when(has2)(pass_own.wait_recv)
    project(2)
    turn_keys(2)

    pl.when(has0)(ahead3.wait_recv)
    earlier_two[0] = jnp.clip(lat[0, block, :], -limit, limit)
    turn_keys(0)

    doc_at = pl.ds(tokens + half, 16)
    doc = lat[3, doc_at, 0:tokens].astype(F32)[0:1, 0:1]
    count = jnp.zeros((1, 1), F32)
    for slot in range(3):
        count += (lat[slot, doc_at, 0:tokens].astype(F32)[0:1, tokens - 1:] == doc).astype(F32)
    wide = (lat[3, doc_at, 0:tokens].astype(F32)[0:1, tokens // 2:tokens // 2 + 1] == doc).astype(F32)
    ahead = z < n_z // 2
    seen[...] = jnp.broadcast_to(count + 4.0 * wide, seen.shape) + jnp.where(ahead, 8.0, 0.0)

    @pl.when(ahead)
    def _():
        project(1)
        project(0)

    rest = z_tops.at[pl.ds(0, n_z - 1)]
    remote(rest, rest, z_send.at[0], z_recv, ctx, me).wait_recv()
    amax_out[...] = jnp.max(z_tops[...], axis=0)

    remote(others, others, own_send, own_recv, ctx, me).wait_send()
    remote(three, three, tops_send, tops_recv, ctx, me).wait_send()
    for k in range(1, n_z):
        pl.when(z - k >= 0)(spread_z(-k).wait_send)
        pl.when(z + k < n_z)(spread_z(k).wait_send)
    earlier(sent)

    @pl.when(next2)
    def _():
        for copy in ahead2:
            copy.wait_send()

    pl.when(next3)(ahead3.wait_send)
    pl.when(core == 0)(pass_own.wait_send)
    pl.when(has1)(on[0][1].wait_send)


def attend(
    gain, seen, own_out, own_top, qn, qx, kt, kx, vals, earlier_two, uk, uv, kt_in, vals_in, amax,
    out, amax_out, kt_two, vals_two, outs, store, amax_store,
):
    heads, hd, width = uk.shape
    tokens = qn.shape[0]
    write_amax = pltpu.make_async_copy(amax, amax_out, amax_store)
    write_amax.start()
    told = jnp.max(seen[...]).astype(jnp.int32)
    code = told & 7
    count = told & 3
    middle = tokens // 2
    together = min(heads, 8)

    def write(p):
        some = pl.ds(pl.multiple_of(p * 4 * hd, 4 * hd), 4 * hd)
        return pltpu.make_async_copy(outs.at[:, some], out.at[:, some], store.at[p])

    for slot in range(2):
        @pl.when((count >= 3 - slot) & (told < 8))
        def _(slot=slot):
            def some(g, carry):
                c = earlier_two[slot]
                ups = nt(uk[pl.ds(4 * g, 4)].reshape(4 * hd, width), c) * gain
                kt_two[slot, pl.ds(4 * g, 4)] = ups.astype(BF16).reshape(4, hd, tokens)
                for p in range(2):
                    h = 4 * g + 2 * p
                    both = nn(c, jnp.concatenate([uv[h], uv[h + 1]], axis=1)).astype(BF16)
                    vals_two[slot, h] = both[:, :hd]
                    vals_two[slot, h + 1] = both[:, hd:]
                return carry

            lax.fori_loop(0, heads // 4, some, 0, unroll=True)

    def with_blocks(blocks, wide):
        seeing = 0 if not blocks else tokens if wide else middle
        skip = middle if wide and blocks == 3 else 0

        def group(g, carry):
            for i in range(together):
                h = together * g + i
                e = i % 2
                cols = pl.ds(pl.multiple_of(h * hd, hd), hd)
                if blocks:
                    q = jnp.concatenate([qn[0:seeing, cols], qx[h, 0:seeing, :]], axis=1)
                    k = [kt_two[x, h] for x in range(3 - blocks, 2)] + [kt[h]]
                    v = [vals_two[x, h] for x in range(3 - blocks, 2)] + [vals[h]]
                    k[0], v[0] = k[0][:, skip:], v[0][skip:]
                    k = jnp.concatenate(k, axis=1)
                    v = jnp.concatenate(v, axis=0)
                    k = jnp.concatenate([k, kx[e, :, (3 - blocks) * tokens + skip:3 * tokens]], axis=0)
                    s = nn(q, k)
                    own = own_top[h, 0:seeing, :]
                    top = jnp.maximum(jnp.broadcast_to(jnp.max(s, axis=1, keepdims=True), own.shape), own)
                    w = jnp.exp2(s - jnp.concatenate([top] * (s.shape[1] // hd), axis=1)).astype(BF16)
                    scale = jnp.exp2(own - top)
                    o = own_out[h, 0:seeing, :] * jnp.concatenate([scale, scale], axis=1) + nn(
                        w, jnp.concatenate([v, jnp.ones(v.shape, BF16)], axis=1)
                    )
                    outs[0:seeing, cols] = (o[:, :hd] / o[:, hd:]).astype(BF16)
                if seeing < tokens:
                    o = own_out[h, seeing:, :]
                    outs[seeing:, cols] = (o[:, :hd] / o[:, hd:]).astype(BF16)
                if i % 4 == 3:
                    write(together // 4 * g + i // 4).start()
            return carry

        lax.fori_loop(0, heads // together, group, 0)

    pl.when(count == 0)(functools.partial(with_blocks, 0, False))
    for blocks in range(1, 4):
        for wide in (False, True):
            pl.when(code == blocks + 4 * wide)(functools.partial(with_blocks, blocks, wide))

    def written(p, carry):
        write(p).wait()
        return carry

    lax.fori_loop(0, heads // 4, written, 0)
    write_amax.wait()


def shards(n_ctx, n_head, q_nope, q_rope, latent, amax_prior, k_rope, w_uk, w_uv, seg_ids):
    tokens, columns = q_nope.shape
    heads, hd, width = w_uk.shape
    rope = k_rope.shape[0]
    rows = latent.shape[0]
    gain = math.log2(math.e) * (hd + rope) ** -0.5
    q_cos, q_sin, k_cos, k_sin = tables(tokens, rope, gain)
    n_z = n_ctx // 4
    keys = BLOCKS * tokens
    dma = pltpu.SemaphoreType.DMA
    anywhere = pl.BlockSpec(memory_space=pl.ANY)
    in_vmem = pl.BlockSpec(memory_space=pltpu.VMEM)
    mib = 1024 * 1024
    operands = (
        latent, amax_prior.reshape(1, width), k_rope, seg_ids.reshape(1, tokens), q_nope, q_rope, w_uk, w_uv,
        jnp.asarray(q_cos), jnp.asarray(q_sin), jnp.asarray(k_cos), jnp.asarray(k_sin),
    )
    results = pl.pallas_call(
        functools.partial(kernel, n_ctx, n_head, gain),
        out_shape=(
            pltpu.VMEM((8, 128), F32),
            pltpu.VMEM((heads, tokens, 2 * hd), F32),
            pltpu.VMEM((heads, tokens, hd), F32),
            pltpu.VMEM((tokens, columns), BF16),
            pltpu.VMEM((heads, tokens, 128), BF16),
            pltpu.VMEM((heads, hd, tokens), BF16),
            pltpu.VMEM((2, 128, keys), BF16),
            pltpu.VMEM((heads, tokens, hd), BF16),
            pltpu.VMEM((2, tokens, width), BF16),
            pltpu.VMEM((heads, hd, width), BF16),
            pltpu.VMEM((heads, width, hd), BF16),
            pltpu.VMEM((2, heads, hd, tokens), BF16),
            pltpu.VMEM((2, heads, tokens, hd), BF16),
            pltpu.VMEM((1, width), F32),
        ),
        in_specs=[pl.BlockSpec(memory_space=pltpu.HBM)] * 12,
        out_specs=(in_vmem,) * 14,
        scratch_shapes=[
            pltpu.VMEM((BLOCKS, tokens + rope // 2 + 16, width), BF16),
            pltpu.VMEM((4, 1, width), F32),
            pltpu.VMEM((n_z, 1, width), F32),
            pltpu.VMEM((1, width), F32),
            pltpu.VMEM((1, tokens), jnp.int32),
            pltpu.VMEM((tokens, heads * rope), BF16),
            pltpu.VMEM(q_cos.shape, F32),
            pltpu.VMEM(q_sin.shape, F32),
            pltpu.VMEM(k_cos.shape, F32),
            pltpu.VMEM(k_sin.shape, F32),
            pltpu.VMEM((tokens, width), BF16),
            pltpu.VMEM((heads, hd, tokens), BF16),
            pltpu.VMEM((heads, tokens, hd), BF16),
            dma,
            dma,
            dma((2, 3)),
            dma((2, 3)),
            dma((2,)),
            dma((2,)),
            dma((2,)),
            dma((2,)),
            dma((3,)),
            dma((BLOCKS,)),
            dma,
            dma,
            dma,
            dma((2 * n_z,)),
            pltpu.SemaphoreType.REGULAR,
            dma((13,)),
        ],
        compiler_params=pltpu.CompilerParams(collective_id=0, has_side_effects=True, vmem_limit_bytes=18 * mib),
        cost_estimate=pl.CostEstimate(flops=4_000_000_000, bytes_accessed=8_000_000, transcendentals=0),
    )(*(pltpu.with_memory_space_constraint(x, pltpu.HBM) for x in operands))
    attended, latent_amax, _, _ = pl.pallas_call(
        functools.partial(attend, gain),
        out_shape=(
            jax.ShapeDtypeStruct((tokens, columns), BF16),
            jax.ShapeDtypeStruct((1, width), F32),
            pltpu.VMEM((2, heads, hd, tokens), BF16),
            pltpu.VMEM((2, heads, tokens, hd), BF16),
        ),
        in_specs=[in_vmem] * 14,
        out_specs=(anywhere, anywhere, in_vmem, in_vmem),
        input_output_aliases={11: 2, 12: 3},
        scratch_shapes=[
            pltpu.VMEM((tokens, columns), BF16),
            dma((heads // 4,)),
            dma,
        ],
        compiler_params=pltpu.CompilerParams(vmem_limit_bytes=18 * mib),
        cost_estimate=pl.CostEstimate(flops=10_000_000_000, bytes_accessed=8_000_000, transcendentals=4_194_304),
    )(*(pltpu.with_memory_space_constraint(x, pltpu.VMEM) for x in results))
    return attended, latent_amax.reshape(width)


def solution(mesh):
    placed = (
        P("ctx", "head"),
        P("ctx", "head"),
        P(("ctx", "head"), None),
        P(),
        P(None, "ctx"),
        P("head", None, None),
        P("head", None, None),
        P("ctx"),
    )
    return jax.shard_map(
        functools.partial(shards, mesh.shape["ctx"], mesh.shape["head"]),
        mesh=mesh, in_specs=placed, out_specs=(P("ctx", "head"), P()), check_vma=False,
    )
```

```python
import functools
import math

import jax
import jax.numpy as jnp
import numpy as np
from jax import lax
from jax.experimental import pallas as pl
from jax.experimental.pallas import tpu as pltpu
from jax.sharding import PartitionSpec as P

MESH = pl.DeviceIdType.MESH
BF16 = jnp.bfloat16
F32 = jnp.float32
BLOCKS = 4
HIDDEN = -1e30


def tables(tokens, rope, gain):
    half = rope // 2
    freq = np.exp(np.arange(half) * (-2.0 * math.log(10000.0) / rope))
    q_angle = np.arange(tokens)[:, None] * freq[None, :]
    q_cos = np.tile(np.cos(q_angle), (1, 4)).astype(np.float32)
    q_sin = np.tile(np.sin(q_angle), (1, 4)).astype(np.float32)
    k_place = np.arange(BLOCKS * tokens) - (BLOCKS - 1) * tokens
    k_angle = freq[:, None] * k_place[None, :]
    k_cos = (np.cos(k_angle) * gain).astype(np.float32)
    k_sin = (np.sin(k_angle) * gain).astype(np.float32)
    return q_cos, q_sin, k_cos, k_sin


def nt(a, b):
    return lax.dot_general(a, b, (((1,), (1,)), ((), ())), preferred_element_type=F32)


def nn(a, b):
    return jnp.dot(a, b, preferred_element_type=F32)


def kernel(
    n_ctx, n_head, gain,
    latent, prior, k_rope, seg, q_nope, q_rope, w_uk, w_uv, q_cos, q_sin, k_cos, k_sin,
    seen, own_out, own_top, qn, qx, kt, kx, vals, earlier_two, uk, uv, kt_two, vals_two, amax_out,
    lat, tops, z_tops, prior_v, seg_v, qr, qc, qs, kc, ks, clipped, kt3, vals3,
    own_recv, own_send, pair_recv, pair_send, side_recv, side_send, far_recv, far_send,
    sib_send, sib_recv, tops_recv, tops_send, z_recv, z_send, hello, load,
):
    ctx = lax.axis_index("ctx")
    me = lax.axis_index("head")
    core = lax.rem(ctx, 2)
    sibling = ctx + 1 - 2 * core
    n_z = n_ctx // 4
    z = ctx // 4
    heads, hd, width = uk.shape
    tokens = qn.shape[0]
    rope = k_rope.shape[0]
    rows = latent.shape[0]
    half = rope // 2
    mine = pl.ds(pl.multiple_of(me * rows, rows), rows)
    block = pl.ds(0, tokens)
    key_rows = pl.ds(tokens, half + 16)

    kind = lax.rem(ctx, 4)
    has1 = ctx >= 2
    has2 = (core == 1) | (ctx >= 2)
    has0 = ctx >= 3
    next2 = ctx + 2 < n_ctx
    next3 = (core == 1) & (ctx + 3 < n_ctx)

    beside = me + 1 - 2 * lax.rem(me, 2)
    up = lax.rem(me + 2, n_head)
    down = lax.rem(me + n_head - 2, n_head)

    def remote(src, dst, send, recv, c, h):
        return pltpu.make_async_remote_copy(
            src_ref=src, dst_ref=dst, send_sem=send, recv_sem=recv, device_id=(c, h), device_id_type=MESH
        )

    loads = [
        (latent, lat.at[3, mine]),
        (k_rope.at[pl.ds(0, half)], lat.at[3, pl.ds(tokens, half), pl.ds(0, tokens)]),
        (k_rope.at[pl.ds(half, half)], lat.at[3, pl.ds(tokens, half), pl.ds(tokens, tokens)]),
        (seg, seg_v), (prior, prior_v),
        (q_rope, qr), (q_cos, qc), (q_sin, qs), (k_cos, kc), (k_sin, ks), (w_uk, uk), (w_uv, uv), (q_nope, qn),
    ]
    loading = [pltpu.make_async_copy(src, dst, load.at[i]) for i, (src, dst) in enumerate(loads)]
    for copy in loading[:10]:
        copy.start()

    barrier = pltpu.get_barrier_semaphore()

    def greet(c, h):
        pl.semaphore_signal(barrier, inc=1, device_id=(c, h), device_id_type=MESH)

    @pl.when(has1)
    def _():
        greet(ctx - 2, me)
        greet(ctx - 2, beside)

    @pl.when((core == 0) & has0)
    def _():
        greet(ctx - 3, me)

    for k in range(1, n_head):
        greet(ctx, lax.rem(me + k, n_head))
    for d in (1, 2, 3):
        greet(4 * z + lax.rem(kind + d, 4), me)
    for k in range(1, n_z):
        pl.when(z + k < n_z)(functools.partial(greet, ctx + 4 * k, me))

    for slot, there in ((0, has0), (1, has1), (2, has2)):
        @pl.when(jnp.logical_not(there))
        def _(slot=slot):
            lat[slot, block, :] = jnp.zeros((tokens, width), BF16)
            lat[slot, key_rows, :] = jnp.full((half + 16, width), -1.0, BF16)

    for copy in loading[:4]:
        copy.wait()
    lat[3, pl.ds(tokens + half, 16), :] = jnp.broadcast_to(
        jnp.concatenate([seg_v[...], seg_v[...]], axis=1).astype(F32), (16, width)
    ).astype(BF16)
    listeners = 2 * next2.astype(jnp.int32) + next3.astype(jnp.int32)
    pl.semaphore_wait(barrier, n_head - 1 + 3 + z + listeners)

    def share(k):
        return remote(
            lat.at[3, mine], lat.at[3, mine], own_send, own_recv, ctx, lax.rem(me + k, n_head)
        )

    def chunk(slot, i, c, h):
        return remote(lat.at[3, mine], lat.at[slot, mine], pair_send.at[slot, i], pair_recv.at[slot, i], c, h)

    def keys_to(slot, c):
        return remote(lat.at[3, key_rows], lat.at[slot, key_rows], pair_send.at[slot, 2], pair_recv.at[slot, 2], c, me)

    ahead2 = [chunk(1, 0, ctx + 2, me), chunk(1, 1, ctx + 2, beside), keys_to(1, ctx + 2)]
    ahead3 = remote(lat.at[3], lat.at[0], sib_send.at[2], sib_recv.at[0], ctx + 3, me)

    for k in range(1, n_head):
        share(k).start()

    @pl.when(next2)
    def _():
        for copy in ahead2:
            copy.start()

    for copy in loading[10:]:
        copy.start()

    for k in range(1, n_z):
        @pl.when(z - k >= 0)
        def _(k=k):
            pl.semaphore_signal(hello, inc=1, device_id=(ctx - 4 * k, me), device_id_type=MESH)

    def pair_at(h):
        return pl.ds(pl.multiple_of(h // 2 * 2 * rows, 2 * rows), 2 * rows)

    def one_at(h, x):
        return pl.ds(pl.multiple_of((h // 2 * 2 + x) * rows, rows), rows)

    def side(slots, i, to):
        at = lat.at[slots, pair_at(me)]
        return remote(at, at, side_send.at[i], side_recv.at[i], ctx, to)

    def far(slots, i, h, to):
        at = lat.at[slots, one_at(h, i)]
        return remote(at, at, far_send.at[i], far_recv.at[i], ctx, to)

    def sides(slots):
        side(slots, 0, up).start()
        side(slots, 1, down).start()

    def fars(slots):
        side(slots, 0, up).wait_recv()
        far(slots, 0, down, up).start()
        side(slots, 1, down).wait_recv()
        far(slots, 1, up, down).start()

    def complete(slots):
        far(slots, 0, down, up).wait_recv()
        far(slots, 1, up, down).wait_recv()

    def sent(slots):
        for i in range(2):
            side(slots, i, up).wait_send()
            far(slots, i, up, up).wait_send()

    late = pl.ds(1, 1)

    def earlier(act):
        pl.when(has1)(functools.partial(act, late))

    @pl.when(has1)
    def _():
        for copy in ahead2:
            copy.wait_recv()

    earlier(sides)

    others = lat.at[3, pl.ds(0, (n_head - 1) * rows)]
    remote(others, others, own_send, own_recv, ctx, me).wait_recv()
    pass_own = remote(lat.at[3], lat.at[2], sib_send.at[0], sib_recv.at[2], sibling, me)
    pl.when(core == 0)(pass_own.start)
    pl.when(next3)(ahead3.start)
    tops[kind] = jnp.max(jnp.abs(lat[3, block, :].astype(F32)), axis=0, keepdims=True)

    def spread_top(d):
        return remote(tops.at[kind], tops.at[kind], tops_send, tops_recv, 4 * z + lax.rem(kind + d, 4), me)

    for d in (1, 2, 3):
        spread_top(d).start()

    for copy in loading[4:10]:
        copy.wait()
    lane = lax.broadcasted_iota(jnp.int32, (tokens, 128), 1)
    docs = lax.broadcasted_iota(jnp.int32, (64, tokens), 0)
    docs = jnp.concatenate([docs, docs], axis=0)
    mark = (docs == jnp.broadcast_to(seg_v[...], (128, tokens))).astype(F32).T
    i = lax.broadcasted_iota(jnp.int32, (128, 128), 0)
    j = lax.broadcasted_iota(jnp.int32, (128, 128), 1)
    low = (j & 63) < 32
    swap = jnp.where(low & (i == j + 32), -1.0, jnp.where(jnp.logical_not(low) & (i == j - 32), 1.0, 0.0)).astype(BF16)
    cosine, sine = qc[...], qs[...]

    def turn(p, carry):
        raw = qr[:, pl.ds(pl.multiple_of(p * 128, 128), 128)]
        turned = raw.astype(F32) * cosine + nn(raw, swap) * sine
        qx[2 * p] = jnp.where(lane < 64, turned, mark).astype(BF16)
        qx[2 * p + 1] = jnp.where(lane < 64, mark, turned).astype(BF16)
        return carry

    lax.fori_loop(0, heads // 2, turn, 0, unroll=True)

    earlier(fars)

    def piece(at):
        return remote(lat.at[1, at], lat.at[2, at], sib_send.at[1], sib_recv.at[2], sibling, me)

    @pl.when((core == 1) & has1)
    def _():
        for at in (pair_at(me), pair_at(up), pair_at(down), key_rows):
            piece(at).start()


    three = tops.at[pl.ds(0, 3)]
    remote(three, three, tops_send, tops_recv, ctx, me).wait_recv()
    z_tops[z] = jnp.max(tops[...], axis=0)

    def spread_z(k):
        return remote(z_tops.at[z], z_tops.at[z], z_send.at[k + n_z], z_recv, ctx + 4 * k, me)

    for k in range(1, n_z):
        pl.when(z - k >= 0)(spread_z(-k).start)

    limit = prior_v[...].astype(BF16)
    for copy in loading[10:]:
        copy.wait()

    def project(slot):
        kt_to, vals_to = (kt3, vals3) if slot == 3 else (kt, vals) if slot == 2 else (kt_two.at[slot], vals_two.at[slot])
        clipped[...] = jnp.clip(lat[slot, block, :], -limit, limit)

        def some(g, carry):
            c = clipped[...]
            ups = (nt(uk[pl.ds(4 * g, 4)].reshape(4 * hd, width), c) * gain).astype(BF16).reshape(4, hd, tokens)
            kt_to[pl.ds(4 * g, 4)] = ups
            for p in range(2):
                h = 4 * g + 2 * p
                both = nn(c, jnp.concatenate([uv[h], uv[h + 1]], axis=1)).astype(BF16)
                for e in range(2):
                    vals_to[h + e] = both[:, e * hd:(e + 1) * hd]
            return carry

        lax.fori_loop(0, heads // 4, some, 0, unroll=True)

    def turn_keys(slot):
        at = pl.ds(slot * tokens, tokens)
        a = lat[slot, pl.ds(tokens, half), 0:tokens].astype(F32)
        b = lat[slot, pl.ds(tokens, half), tokens:2 * tokens].astype(F32)
        cosine, sine = kc[:, at], ks[:, at]
        turned = jnp.concatenate([a * cosine - b * sine, b * cosine + a * sine], axis=0).astype(BF16)
        doc = jnp.broadcast_to(lat[slot, pl.ds(tokens + half, 16), 0:tokens].astype(F32)[0:1, :], (64, tokens))
        number = lax.broadcasted_iota(jnp.int32, (64, tokens), 0).astype(F32)
        other = jnp.where(doc == number, 0.0, HIDDEN).astype(BF16)
        kx[0, 0:64, at] = turned
        kx[0, 64:128, at] = other
        kx[1, 0:64, at] = other
        kx[1, 64:128, at] = turned

    project(3)

    turn_keys(3)

    earlier(complete)
    to_core1 = remote(lat.at[1], lat.at[0], sib_send.at[1], sib_recv.at[0], sibling, me)
    pl.when((core == 0) & has1)(to_core1.start)
    pl.when((core == 1) & has1)(piece(pair_at(lax.rem(me + 4, n_head))).start)

    q_at = lax.broadcasted_iota(jnp.int32, (tokens, tokens), 0)
    k_at = lax.broadcasted_iota(jnp.int32, (tokens, tokens), 1)

    def attend_own(first):
        for h in range(first, first + heads // 2):
            q = jnp.concatenate([qn[:, h * hd:(h + 1) * hd], qx[h]], axis=1)
            k = jnp.concatenate([kt3[h], kx[h % 2, :, 3 * tokens:]], axis=0)
            s = jnp.where(k_at <= q_at, nn(q, k), HIDDEN)
            top = jnp.max(s, axis=1, keepdims=True)
            w = jnp.exp2(s - top).astype(BF16)
            own_out[h] = nn(w, jnp.concatenate([vals3[h], jnp.ones((tokens, hd), BF16)], axis=1))
            own_top[h] = jnp.broadcast_to(top, (tokens, hd))

    attend_own(0)

    @pl.when(z < n_z - 1)
    def _():
        pl.semaphore_wait(hello, n_z - 1 - z)
        for k in range(1, n_z):
            pl.when(z + k < n_z)(spread_z(k).start)

    attend_own(heads // 2)

    earlier_two[1] = jnp.clip(lat[1, block, :], -limit, limit)
    turn_keys(1)

    pl.when(has2)(pass_own.wait_recv)
    project(2)
    turn_keys(2)

    pl.when(has0)(ahead3.wait_recv)
    earlier_two[0] = jnp.clip(lat[0, block, :], -limit, limit)
    turn_keys(0)

    doc_at = pl.ds(tokens + half, 16)
    doc = lat[3, doc_at, 0:tokens].astype(F32)[0:1, 0:1]
    count = jnp.zeros((1, 1), F32)
    for slot in range(3):
        count += (lat[slot, doc_at, 0:tokens].astype(F32)[0:1, tokens - 1:] == doc).astype(F32)
    wide = (lat[3, doc_at, 0:tokens].astype(F32)[0:1, tokens // 2:tokens // 2 + 1] == doc).astype(F32)
    ahead = z < n_z // 2
    seen[...] = jnp.broadcast_to(count + 4.0 * wide, seen.shape) + jnp.where(ahead, 8.0, 0.0)

    @pl.when(ahead)
    def _():
        project(1)
        project(0)

    rest = z_tops.at[pl.ds(0, n_z - 1)]
    remote(rest, rest, z_send.at[0], z_recv, ctx, me).wait_recv()
    amax_out[...] = jnp.max(z_tops[...], axis=0)

    remote(others, others, own_send, own_recv, ctx, me).wait_send()
    remote(three, three, tops_send, tops_recv, ctx, me).wait_send()
    for k in range(1, n_z):
        pl.when(z - k >= 0)(spread_z(-k).wait_send)
        pl.when(z + k < n_z)(spread_z(k).wait_send)
    earlier(sent)

    @pl.when(next2)
    def _():
        for copy in ahead2:
            copy.wait_send()

    pl.when(next3)(ahead3.wait_send)
    pl.when(core == 0)(pass_own.wait_send)
    pl.when(has1)(to_core1.wait_send)


def attend(
    gain, seen, own_out, own_top, qn, qx, kt, kx, vals, earlier_two, uk, uv, kt_in, vals_in, amax,
    out, amax_out, kt_two, vals_two, outs, store, amax_store,
):
    heads, hd, width = uk.shape
    tokens = qn.shape[0]
    write_amax = pltpu.make_async_copy(amax, amax_out, amax_store)
    write_amax.start()
    told = jnp.max(seen[...]).astype(jnp.int32)
    code = told & 7
    count = told & 3
    middle = tokens // 2
    together = min(heads, 8)

    def write(p):
        some = pl.ds(pl.multiple_of(p * 4 * hd, 4 * hd), 4 * hd)
        return pltpu.make_async_copy(outs.at[:, some], out.at[:, some], store.at[p])

    for slot in range(2):
        @pl.when((count >= 3 - slot) & (told < 8))
        def _(slot=slot):
            def some(g, carry):
                c = earlier_two[slot]
                ups = nt(uk[pl.ds(4 * g, 4)].reshape(4 * hd, width), c) * gain
                kt_two[slot, pl.ds(4 * g, 4)] = ups.astype(BF16).reshape(4, hd, tokens)
                for p in range(2):
                    h = 4 * g + 2 * p
                    both = nn(c, jnp.concatenate([uv[h], uv[h + 1]], axis=1)).astype(BF16)
                    vals_two[slot, h] = both[:, :hd]
                    vals_two[slot, h + 1] = both[:, hd:]
                return carry

            lax.fori_loop(0, heads // 4, some, 0, unroll=True)

    def with_blocks(blocks, wide):
        seeing = 0 if not blocks else tokens if wide else middle
        skip = middle if wide and blocks == 3 else 0

        def group(g, carry):
            for i in range(together):
                h = together * g + i
                e = i % 2
                cols = pl.ds(pl.multiple_of(h * hd, hd), hd)
                if blocks:
                    q = jnp.concatenate([qn[0:seeing, cols], qx[h, 0:seeing, :]], axis=1)
                    k = [kt_two[x, h] for x in range(3 - blocks, 2)] + [kt[h]]
                    v = [vals_two[x, h] for x in range(3 - blocks, 2)] + [vals[h]]
                    k[0], v[0] = k[0][:, skip:], v[0][skip:]
                    k = jnp.concatenate(k, axis=1)
                    v = jnp.concatenate(v, axis=0)
                    k = jnp.concatenate([k, kx[e, :, (3 - blocks) * tokens + skip:3 * tokens]], axis=0)
                    s = nn(q, k)
                    own = own_top[h, 0:seeing, :]
                    top = jnp.maximum(jnp.broadcast_to(jnp.max(s, axis=1, keepdims=True), own.shape), own)
                    w = jnp.exp2(s - jnp.concatenate([top] * (s.shape[1] // hd), axis=1)).astype(BF16)
                    scale = jnp.exp2(own - top)
                    o = own_out[h, 0:seeing, :] * jnp.concatenate([scale, scale], axis=1) + nn(
                        w, jnp.concatenate([v, jnp.ones(v.shape, BF16)], axis=1)
                    )
                    outs[0:seeing, cols] = (o[:, :hd] / o[:, hd:]).astype(BF16)
                if seeing < tokens:
                    o = own_out[h, seeing:, :]
                    outs[seeing:, cols] = (o[:, :hd] / o[:, hd:]).astype(BF16)
                if i % 4 == 3:
                    write(together // 4 * g + i // 4).start()
            return carry

        lax.fori_loop(0, heads // together, group, 0)

    pl.when(count == 0)(functools.partial(with_blocks, 0, False))
    for blocks in range(1, 4):
        for wide in (False, True):
            pl.when(code == blocks + 4 * wide)(functools.partial(with_blocks, blocks, wide))

    def written(p, carry):
        write(p).wait()
        return carry

    lax.fori_loop(0, heads // 4, written, 0)
    write_amax.wait()


def shards(n_ctx, n_head, q_nope, q_rope, latent, amax_prior, k_rope, w_uk, w_uv, seg_ids):
    tokens, columns = q_nope.shape
    heads, hd, width = w_uk.shape
    rope = k_rope.shape[0]
    rows = latent.shape[0]
    gain = math.log2(math.e) * (hd + rope) ** -0.5
    q_cos, q_sin, k_cos, k_sin = tables(tokens, rope, gain)
    n_z = n_ctx // 4
    keys = BLOCKS * tokens
    dma = pltpu.SemaphoreType.DMA
    anywhere = pl.BlockSpec(memory_space=pl.ANY)
    in_vmem = pl.BlockSpec(memory_space=pltpu.VMEM)
    mib = 1024 * 1024
    operands = (
        latent, amax_prior.reshape(1, width), k_rope, seg_ids.reshape(1, tokens), q_nope, q_rope, w_uk, w_uv,
        jnp.asarray(q_cos), jnp.asarray(q_sin), jnp.asarray(k_cos), jnp.asarray(k_sin),
    )
    results = pl.pallas_call(
        functools.partial(kernel, n_ctx, n_head, gain),
        out_shape=(
            pltpu.VMEM((8, 128), F32),
            pltpu.VMEM((heads, tokens, 2 * hd), F32),
            pltpu.VMEM((heads, tokens, hd), F32),
            pltpu.VMEM((tokens, columns), BF16),
            pltpu.VMEM((heads, tokens, 128), BF16),
            pltpu.VMEM((heads, hd, tokens), BF16),
            pltpu.VMEM((2, 128, keys), BF16),
            pltpu.VMEM((heads, tokens, hd), BF16),
            pltpu.VMEM((2, tokens, width), BF16),
            pltpu.VMEM((heads, hd, width), BF16),
            pltpu.VMEM((heads, width, hd), BF16),
            pltpu.VMEM((2, heads, hd, tokens), BF16),
            pltpu.VMEM((2, heads, tokens, hd), BF16),
            pltpu.VMEM((1, width), F32),
        ),
        in_specs=[pl.BlockSpec(memory_space=pltpu.HBM)] * 12,
        out_specs=(in_vmem,) * 14,
        scratch_shapes=[
            pltpu.VMEM((BLOCKS, tokens + rope // 2 + 16, width), BF16),
            pltpu.VMEM((4, 1, width), F32),
            pltpu.VMEM((n_z, 1, width), F32),
            pltpu.VMEM((1, width), F32),
            pltpu.VMEM((1, tokens), jnp.int32),
            pltpu.VMEM((tokens, heads * rope), BF16),
            pltpu.VMEM(q_cos.shape, F32),
            pltpu.VMEM(q_sin.shape, F32),
            pltpu.VMEM(k_cos.shape, F32),
            pltpu.VMEM(k_sin.shape, F32),
            pltpu.VMEM((tokens, width), BF16),
            pltpu.VMEM((heads, hd, tokens), BF16),
            pltpu.VMEM((heads, tokens, hd), BF16),
            dma,
            dma,
            dma((2, 3)),
            dma((2, 3)),
            dma((2,)),
            dma((2,)),
            dma((2,)),
            dma((2,)),
            dma((3,)),
            dma((BLOCKS,)),
            dma,
            dma,
            dma,
            dma((2 * n_z,)),
            pltpu.SemaphoreType.REGULAR,
            dma((13,)),
        ],
        compiler_params=pltpu.CompilerParams(collective_id=0, has_side_effects=True, vmem_limit_bytes=18 * mib),
        cost_estimate=pl.CostEstimate(flops=4_000_000_000, bytes_accessed=8_000_000, transcendentals=0),
    )(*(pltpu.with_memory_space_constraint(x, pltpu.HBM) for x in operands))
    attended, latent_amax, _, _ = pl.pallas_call(
        functools.partial(attend, gain),
        out_shape=(
            jax.ShapeDtypeStruct((tokens, columns), BF16),
            jax.ShapeDtypeStruct((1, width), F32),
            pltpu.VMEM((2, heads, hd, tokens), BF16),
            pltpu.VMEM((2, heads, tokens, hd), BF16),
        ),
        in_specs=[in_vmem] * 14,
        out_specs=(anywhere, anywhere, in_vmem, in_vmem),
        input_output_aliases={11: 2, 12: 3},
        scratch_shapes=[
            pltpu.VMEM((tokens, columns), BF16),
            dma((heads // 4,)),
            dma,
        ],
        compiler_params=pltpu.CompilerParams(vmem_limit_bytes=18 * mib),
        cost_estimate=pl.CostEstimate(flops=10_000_000_000, bytes_accessed=8_000_000, transcendentals=4_194_304),
    )(*(pltpu.with_memory_space_constraint(x, pltpu.VMEM) for x in results))
    return attended, latent_amax.reshape(width)


def solution(mesh):
    placed = (
        P("ctx", "head"),
        P("ctx", "head"),
        P(("ctx", "head"), None),
        P(),
        P(None, "ctx"),
        P("head", None, None),
        P("head", None, None),
        P("ctx"),
    )
    return jax.shard_map(
        functools.partial(shards, mesh.shape["ctx"], mesh.shape["head"]),
        mesh=mesh, in_specs=placed, out_specs=(P("ctx", "head"), P()), check_vma=False,
    )
```
